32 devices in a mesh: prompt: 4 (over z), decode: 8 (over y, x, core).
Axes of the slice: x: 2, y: 2, z: 4, core: 2. Of those that a mesh axis runs over, the one named last changes fastest.
Arguments:
- hidden_in: bfloat16 [16, 32, 4096], P('prompt', 'decode'), may hold values from -6 to 6
- queries: bfloat16 [16, 32, 4096], P('prompt', 'decode'), may hold values from -8 to 8
- new_kv: bfloat16 [16, 32, 512], P('prompt', 'decode'), may hold values from -8 to 8
- prompt_kv: bfloat16 [16, 4096, 512], P('prompt', 'decode'), may hold values from -8 to 8
- sample_kv: bfloat16 [16, 32, 64, 512], P('prompt', 'decode'), may hold values from -8 to 8
- counts: int32 [16, 32], P('prompt', 'decode'), may hold values from 1 to 64, 1024 in all within a row
- out_proj: bfloat16 [4096, 4096], P('decode'), may hold values from -0.5 to 0.5
- norm_gain: float32 [4096], replicated, may hold values from 0.5 to 1.5
- expert_ids: int32 [4, 8, 16, 8], P('prompt', 'decode'), may hold values from 0 to 31, all different within a row; in each aligned block of 16 rows (0 to 15, 16 to 31, ..., all dimensions but the last counted through in order) at most 8 rows name the same one
- expert_gates: float32 [4, 8, 16, 8], P('prompt', 'decode'), may hold values from 0.05 to 0.35
- w_gate: bfloat16 [32, 4096, 768], P(('prompt', 'decode')), may hold values from -0.09375 to 0.09375
- w_up: bfloat16 [32, 4096, 768], P(('prompt', 'decode')), may hold values from -0.09375 to 0.09375
- w_down: bfloat16 [32, 768, 4096], P(('prompt', 'decode')), may hold values from -0.21875 to 0.21875
Outputs:
- mixed: bfloat16 [16, 32, 4096], P('prompt', 'decode')
The draws below stay inside these ranges and needn't reach their ends.
Inputs may be any that keep to these rules, and one draw needn't show every extreme that they name: `expert_ids`: each row names 8 different experts; among the 16 rows of one [a, b] block no expert is named more than 8 times, and in some block some expert exactly 8 times. `counts`: for every prompt the largest count is 64.
All inputs are finite; a program needn't handle non-finite values. No bound on the sum of `counts` on one device may be relied on, other than what follows from the above.
Results may differ from the reference program's by a relative error of at most 0.0073.
Values may be sent and summed in bfloat16 or wider, within the bound.
A program may use at most 128 MiB of HBM per device.

```python
import math
import jax
import jax.numpy as jnp
import numpy as np
from jax import lax

D = 4096
H = 32
KVH = 2
HD = 128
FF = 768
TOPK = 8
P_DEV = 4
S_DEV = 4
LEN = 4096
GEN = 64
ROWS_DEV = 16
PROMPTS = 16
SAMPLES = 32
BLOCK = 512
EXPERTS = 32
CAP = 8
N_PROMPT = 4
N_DECODE = 8
DEVICES = 32


def draw_queries(key, part):
    key = jax.random.fold_in(key, 5)
    base_key = jax.random.fold_in(key, 0)
    values = 2.0 * jax.random.truncated_normal(base_key, -4.0, 4.0, (PROMPTS, SAMPLES, H, HD), jnp.float32)
    return values.reshape(PROMPTS, SAMPLES, H * HD).astype(jnp.bfloat16)


def draw_prompt_kv(key, part):
    key = jax.random.fold_in(key, 9)
    first_key, second_key = jax.random.split(key, 2)
    keys_part = jax.random.truncated_normal(first_key, -4.0, 4.0, (PROMPTS, LEN, KVH, HD), jnp.float32)
    values_part = jax.random.truncated_normal(second_key, -4.0, 4.0, (PROMPTS, LEN, KVH, HD), jnp.float32)
    joined = jnp.concatenate([keys_part.reshape(PROMPTS, LEN, KVH * HD), values_part.reshape(PROMPTS, LEN, KVH * HD)], axis=-1)
    return joined.astype(jnp.bfloat16)


def draw_sample_kv(key, part):
    key = jax.random.fold_in(key, 13)
    values = jax.random.truncated_normal(key, -6.0, 6.0, (PROMPTS, SAMPLES, GEN, 2, KVH, HD), jnp.float32)
    return values.reshape(PROMPTS, SAMPLES, GEN, 2 * KVH * HD).astype(jnp.bfloat16)


def draw_new_kv(key, part):
    key = jax.random.fold_in(key, 17)
    values = jax.random.truncated_normal(key, -6.0, 6.0, (PROMPTS, SAMPLES, 2, KVH, HD), jnp.float32)
    return values.reshape(PROMPTS, SAMPLES, 2 * KVH * HD).astype(jnp.bfloat16)


def steps_of(own_key, shape, cuts, low, high):
    loudness, own = 1.0, jax.random.fold_in(own_key, 6)
    for axis_at, shards_of in cuts:
        draws = jnp.exp(jax.random.uniform(jax.random.fold_in(own, axis_at), (shards_of,), jnp.float32, low / len(cuts), high / len(cuts)))
        loudness = loudness * jnp.repeat(draws, shape[axis_at] // shards_of).reshape([-1 if axis == axis_at else 1 for axis in range(len(shape))])
    return loudness


def length_profile(number_of, total, most, skew):
    portions = [(1 << 20) // math.isqrt(standing ** skew) + 1 for standing in range(2, number_of + 1)]
    rest, given = total - most - (number_of - 1), [1] * (number_of - 1)
    while rest > 0:
        free = [i for i in range(number_of - 1) if given[i] < most]
        mass, left = sum([portions[i] for i in free]), rest
        for i in free:
            extra = min(most - given[i], max(1, left * portions[i] // mass), rest)
            given[i] = given[i] + extra
            rest = rest - extra
    return np.array([most] + given)


def uneven_parts(stream_key, count, total, reach, lean):
    if count == 2:
        one = jax.random.randint(stream_key, (), max(1, total - reach), min(reach, total - 1) + 1)
        return jnp.stack([one, total - one])
    sizes = jnp.asarray(length_profile(count, total, reach, lean), jnp.int32)
    couples = (count - 1) // 2
    giver, taker = sizes[1:1 + 2 * couples:2], sizes[2:2 + 2 * couples:2]
    margin = jnp.minimum(giver - 1, reach - taker)
    passed = jax.random.randint(jax.random.fold_in(stream_key, 1), (couples,), 0, 1 << 20) % (margin + 1)
    sizes = sizes.at[1:1 + 2 * couples:2].set(giver - passed).at[2:2 + 2 * couples:2].set(taker + passed)
    return sizes[jax.random.permutation(jax.random.fold_in(stream_key, 2), count)]


def deal_out(own_key, own, number, rows, amount, top, most, lean):
    sequence = jax.random.permutation(own_key, amount)
    heavy_load, common = load_shares(amount, rows * top, most, lean, True), load_shares(amount, rows * top, most, lean, False)
    places = jnp.arange(amount)

    def named(sizes, turn):
        used = int((sizes > 0).sum())
        fixed = max(1, used // 4)
        moved = fixed + (places - fixed + turn * (used - fixed)) % max(1, amount - fixed)
        return jnp.zeros((amount,), jnp.int32).at[sequence[jnp.where(places < fixed, places, moved)]].set(jnp.asarray(sizes, jnp.int32))

    sizes = jnp.where(number % 4 == 0, named(heavy_load, number // 4), named(common, number - number // 4 - 1))
    mixed = jax.random.permutation(jax.random.fold_in(own, 3), amount)
    giver, taker = mixed[0:amount // 2 * 2:2], mixed[1:amount // 2 * 2:2]
    slack = jnp.minimum(sizes[giver] - 1, most - sizes[taker]) // 2
    slack = jnp.where((giver == sequence[0]) | (taker == sequence[0]) | (sizes[taker] == 0), 0, jnp.maximum(slack, 0))
    moved = jax.random.randint(jax.random.fold_in(own, 4), (amount // 2,), 0, 1 << 20) % (slack + 1)
    sizes = sizes.at[giver].add(-moved).at[taker].add(moved)
    items = jnp.searchsorted(jnp.cumsum(sizes), jnp.arange(rows * top), side="right").astype(jnp.int32)
    table = items.reshape(top, rows).T
    table = table[jax.random.permutation(jax.random.fold_in(own, 1), rows)]
    turn = jax.random.randint(jax.random.fold_in(own, 2), (rows, 1), 0, top)
    return jnp.take_along_axis(table, (jnp.arange(top)[None, :] + turn) % top, axis=1)


def load_shares(number_of, total, reach, slope, full):
    portions = [(1 << 20) // math.isqrt(standing ** slope) + 1 for standing in range(1, number_of + 1)]
    largest = reach if full else min(reach, max(-(-total // number_of), total * portions[0] // sum(portions)))
    least = 1 if total - largest >= number_of - 1 else 0
    given, surplus = [largest] + [least] * (number_of - 1), total - largest - least * (number_of - 1)
    while surplus > 0:
        free = [i for i in range(1, number_of) if given[i] < largest] or [i for i in range(1, number_of) if given[i] < reach]
        whole, budget = sum([portions[i] for i in free]), surplus
        for i in free:
            extra = min(reach - given[i], max(1, budget * portions[i] // whole), surplus)
            given[i] = given[i] + extra
            surplus = surplus - extra
    return np.array(given)


def gaussian(stream_key, extent, scale, most, cuts=(), kind=jnp.bfloat16):
    entries = jax.random.normal(stream_key, extent, jnp.float32) * scale
    if len(cuts) > 0:
        entries = steps_of(stream_key, extent, cuts, -0.22, 0.18) * entries
    return jnp.clip(entries, min=-most, max=most).astype(kind)


def setup_inputs(seed: int = 0) -> dict:
    keys = jax.random.split(jax.random.key(seed), 14)
    hidden_in = gaussian(keys[0], (PROMPTS, SAMPLES, D), 1.0, 6.0, ((0, 4), (1, 8)))
    queries = draw_queries(jax.random.fold_in(keys[13], 71), 0)
    new_kv = draw_new_kv(jax.random.fold_in(keys[13], 71), 0)
    prompt_kv = draw_prompt_kv(jax.random.fold_in(keys[13], 71), 0)
    sample_kv = draw_sample_kv(jax.random.fold_in(keys[13], 71), 0)
    counts = jax.vmap(lambda own: uneven_parts(own, SAMPLES, SAMPLES * GEN // 2, GEN, 2))(jax.random.split(keys[5], PROMPTS)).reshape((PROMPTS, SAMPLES)).astype(jnp.int32)
    out_proj = gaussian(keys[6], (H * HD, D), HD ** -0.5, 0.5, ((0, 8),))
    norm_gain = jnp.clip(1.0 + 0.1 * jax.random.normal(keys[7], (D,), jnp.float32), 0.5, 1.5)
    expert_ids_keys = jax.random.split(jax.random.fold_in(keys[8], 1), N_PROMPT * N_DECODE * ROWS_DEV // ROWS_DEV)
    expert_ids_turns = jax.random.permutation(jax.random.fold_in(keys[8], 3), N_PROMPT * N_DECODE * ROWS_DEV // ROWS_DEV)
    expert_ids = jax.vmap(lambda own, number: deal_out(jax.random.fold_in(keys[8], 2), own, number, ROWS_DEV, EXPERTS, TOPK, CAP, 2))(expert_ids_keys, expert_ids_turns).reshape((N_PROMPT, N_DECODE, ROWS_DEV, TOPK))
    expert_gates = jnp.clip(0.05 + 0.29999999 * jax.random.uniform(keys[9], (N_PROMPT, N_DECODE, ROWS_DEV, TOPK), jnp.float32) ** steps_of(keys[9], (N_PROMPT, N_DECODE, ROWS_DEV, TOPK), ((0, 4), (1, 8)), -0.2, 0.2), 0.05, 0.35)
    w_gate = gaussian(keys[10], (EXPERTS, D, FF), D ** -0.5, 0.09375, ((0, 32),))
    w_up = gaussian(keys[11], (EXPERTS, D, FF), D ** -0.5, 0.09375, ((0, 32),))
    w_down = gaussian(keys[12], (EXPERTS, FF, D), FF ** -0.5, 0.21875, ((0, 32),))
    return dict(hidden_in=hidden_in, queries=queries, new_kv=new_kv, prompt_kv=prompt_kv, sample_kv=sample_kv, counts=counts, out_proj=out_proj, norm_gain=norm_gain, expert_ids=expert_ids, expert_gates=expert_gates, w_gate=w_gate, w_up=w_up, w_down=w_down)


very_low = -1e+30

def expert_ffn(rows_in, gate_matrix, up_matrix, down_matrix):
    gated = jnp.dot(rows_in, gate_matrix, preferred_element_type=jnp.float32)
    lifted = jnp.dot(rows_in, up_matrix, preferred_element_type=jnp.float32)
    hidden_act = (jax.nn.silu(gated) * lifted).astype(jnp.bfloat16)
    return jnp.dot(hidden_act, down_matrix, preferred_element_type=jnp.float32).astype(jnp.bfloat16)

def reference(hidden_in, queries, new_kv, prompt_kv, sample_kv, counts, out_proj, norm_gain, expert_ids, expert_gates, w_gate, w_up, w_down):
    groups = H // KVH
    score_scale = HD ** (-0.5)
    half = KVH * HD

    def one_prompt(pieces):
        query_rows, page_rows, cache_rows, fresh_rows, lengths = pieces
        grouped = query_rows.astype(jnp.float32).reshape(SAMPLES, KVH, groups, HD)
        key_part = page_rows[:, :half].astype(jnp.float32).reshape(N_DECODE, BLOCK, KVH, HD)
        value_part = page_rows[:, half:].astype(jnp.float32).reshape(N_DECODE, BLOCK, KVH, HD)
        scores = jnp.einsum('skgd,cbkd->cskgb', grouped, key_part) * score_scale
        maxima = lax.optimization_barrier(jnp.max(scores, axis=-1))
        weights = jnp.exp(scores - maxima[..., None])
        totals = lax.optimization_barrier(jnp.sum(weights, axis=-1))
        rounded = lax.optimization_barrier(weights.astype(jnp.bfloat16)).astype(jnp.float32)
        block_out = (jnp.einsum('cskgb,cbkd->cskgd', rounded, value_part) / totals[..., None]).astype(jnp.bfloat16)
        cache_keys = cache_rows[..., :half].astype(jnp.float32).reshape(SAMPLES, GEN, KVH, HD)
        cache_values = cache_rows[..., half:].astype(jnp.float32).reshape(SAMPLES, GEN, KVH, HD)
        fresh_key = fresh_rows[:, :half].astype(jnp.float32).reshape(SAMPLES, KVH, HD)
        fresh_value = fresh_rows[:, half:].astype(jnp.float32).reshape(SAMPLES, KVH, HD)
        own_scores = jnp.einsum('skgd,stkd->skgt', grouped, cache_keys) * score_scale
        fresh_score = jnp.einsum('skgd,skd->skg', grouped, fresh_key) * score_scale
        keep_mask = (jnp.arange(GEN, dtype=jnp.int32)[None, :] < lengths.astype(jnp.int32)[:, None])[:, None, None, :]
        masked = jnp.where(keep_mask, own_scores, very_low)
        own_max = jnp.maximum(lax.optimization_barrier(jnp.max(masked, axis=-1)), fresh_score)
        own_weights = jnp.exp(masked - own_max[..., None])
        fresh_weight = jnp.exp(fresh_score - own_max)
        own_totals = lax.optimization_barrier(jnp.sum(own_weights, axis=-1)) + fresh_weight
        rounded_own = lax.optimization_barrier(own_weights.astype(jnp.bfloat16)).astype(jnp.float32)
        rounded_fresh = lax.optimization_barrier(fresh_weight.astype(jnp.bfloat16)).astype(jnp.float32)
        own_out = jnp.einsum('skgt,stkd->skgd', rounded_own, cache_values) + rounded_fresh[..., None] * fresh_value[:, :, None, :]
        own_out = (own_out / own_totals[..., None]).astype(jnp.bfloat16)
        outputs = jnp.concatenate([block_out, own_out[None]], axis=0).astype(jnp.float32)
        all_max = jnp.concatenate([maxima, own_max[None]], axis=0)
        all_totals = jnp.concatenate([totals, own_totals[None]], axis=0)
        best = lax.optimization_barrier(jnp.max(all_max, axis=0))
        factors = jnp.exp(all_max - best[None]) * all_totals
        joined = lax.optimization_barrier(jnp.sum(factors[..., None] * outputs, axis=0)) / lax.optimization_barrier(jnp.sum(factors, axis=0))[..., None]
        return joined.astype(jnp.bfloat16).reshape(SAMPLES, H * HD)
    attention = lax.map(one_prompt, (queries, prompt_kv, sample_kv, new_kv, counts))
    flat_rows = PROMPTS * SAMPLES
    residual_sum = hidden_in.reshape(flat_rows, D).astype(jnp.float32) + jnp.dot(attention.reshape(flat_rows, H * HD), out_proj, preferred_element_type=jnp.float32)
    normed = (residual_sum * lax.rsqrt(lax.optimization_barrier(jnp.mean(residual_sum * residual_sum, axis=-1, keepdims=True)) + 1e-06) * norm_gain).astype(jnp.bfloat16)
    chosen = expert_ids.reshape(N_PROMPT, N_DECODE, P_DEV, S_DEV, TOPK).transpose(0, 2, 1, 3, 4).reshape(flat_rows * TOPK)
    gate_flat = expert_gates.reshape(N_PROMPT, N_DECODE, P_DEV, S_DEV, TOPK).transpose(0, 2, 1, 3, 4).reshape(flat_rows * TOPK)
    assigned = flat_rows * TOPK
    row_of = jnp.arange(assigned, dtype=jnp.int32) // TOPK
    most_rows = CAP * DEVICES

    def one_expert(accumulated, expert):
        hits = chosen == expert
        place = jnp.cumsum(hits.astype(jnp.int32)) - 1
        target = jnp.where(hits, place, most_rows).astype(jnp.int32)
        listing = jnp.zeros((most_rows,), jnp.int32).at[target].set(jnp.arange(assigned, dtype=jnp.int32), mode='drop')
        valid = jnp.arange(most_rows, dtype=jnp.int32) < jnp.sum(hits.astype(jnp.int32))
        picked_rows = row_of[listing]
        row_weights = jnp.where(valid, gate_flat[listing], 0.0)
        result = expert_ffn(normed[picked_rows], w_gate[expert], w_up[expert], w_down[expert])
        accumulated = accumulated.at[picked_rows].add(row_weights[:, None] * result.astype(jnp.float32))
        return (accumulated, None)
    blended = lax.scan(one_expert, jnp.zeros((flat_rows, D), jnp.float32), jnp.arange(EXPERTS, dtype=jnp.int32))[0]
    return (residual_sum + blended).astype(jnp.bfloat16).reshape(PROMPTS, SAMPLES, D)
```

```python
import functools

import jax
import jax.numpy as jnp
from jax import lax
from jax.experimental import pallas as pl
from jax.experimental.pallas import tpu as pltpu
from jax.sharding import PartitionSpec as P

H = 32
KVH = 2
HD = 128
TOPK = 8
GROUPS = H // KVH
SCALE = HD ** (-0.5)
LOW = -1e30
MESH = pl.DeviceIdType.MESH
BF = jnp.bfloat16
F32 = jnp.float32


def nbits(n):
    return n.bit_length() - 1


def bit_of(axis, k):
    return lax.rem(lax.axis_index(axis) // (1 << k), 2)


def partner(axis, k):
    me = lax.axis_index(axis)
    return {axis: me + (1 - 2 * bit_of(axis, k)) * (1 << k)}


def cube_index(dims, fixed, flip=None):
    out = []
    for dim in dims:
        if dim == flip:
            out.append(1 - bit_of(*dim))
        elif dim in fixed:
            out.append(bit_of(*dim))
        else:
            out.append(slice(None))
    return tuple(out)


def gather_copy(ref, dims, order, step, tail, ssem, rsem):
    fixed = set(order[step:])
    view = ref.at[cube_index(dims, fixed) + tail]
    return pltpu.make_async_remote_copy(
        src_ref=view, dst_ref=view, send_sem=ssem, recv_sem=rsem,
        device_id=partner(*order[step]), device_id_type=MESH,
    )


def scatter_copy(ref, land, dims, order, step, tail, ssem, rsem):
    fixed = set(order[:step])
    view = ref.at[cube_index(dims, fixed, flip=order[step]) + tail]
    return pltpu.make_async_remote_copy(
        src_ref=view, dst_ref=land, send_sem=ssem, recv_sem=rsem,
        device_id=partner(*order[step]), device_id_type=MESH,
    )


def attention_kernel(
    nd, hpd, tdt,
    q_ref, kv_ref, skv_ref, nkv_ref, bias_ref, wo_ref, hid_ref, gain_ref, gates_ref,
    res_ref, pay_ref,
    qall, kv, skv, wo, obuf, orecv, stat, strecv, acc, *rest,
):
    nb = nbits(nd)
    lands = [rest[:nb], rest[nb : 2 * nb]]
    local_sem, q_s, q_r, o_s, o_r, t_s, t_r, p_s, p_r = rest[2 * nb :]
    me = lax.axis_index("decode")
    dims = [("decode", k) for k in range(nb - 1, -1, -1)]
    orders = [dims[:-1][::-1] + dims[-1:], dims[:-1] + dims[-1:]]
    tile = hpd * 4
    kv_heads_dev = GROUPS // hpd

    loads = [
        pltpu.make_async_copy(skv_ref, skv, local_sem.at[0]),
        pltpu.make_async_copy(kv_ref, kv, local_sem.at[1]),
        pltpu.make_async_copy(wo_ref, wo, local_sem.at[2]),
    ]
    for load in loads:
        load.start()

    barrier = pltpu.get_barrier_semaphore()
    for k in range(1, nd):
        pl.semaphore_signal(
            barrier, inc=1, device_id={"decode": lax.rem(me + k, nd)}, device_id_type=MESH
        )
    mine = cube_index(dims, set(dims))
    for part in range(2):
        qall[(part,) + mine] = q_ref[2 * part : 2 * part + 2]
    pl.semaphore_wait(barrier, nd - 1)

    def q_copy(part, step):
        return gather_copy(
            qall.at[part], dims, orders[part], step, (), q_s.at[part, step], q_r.at[part, step]
        )

    for part in range(2):
        q_copy(part, 0).start()

    loads[0].wait()
    for g in range(KVH):
        ks, vs = slice(g * HD, (g + 1) * HD), slice((KVH + g) * HD, (KVH + g + 1) * HD)
        pad = jnp.zeros((112, HD), BF)
        keys = jnp.concatenate([skv[:, ks], nkv_ref[:, ks], pad], axis=0)
        values = jnp.concatenate([skv[:, vs], nkv_ref[:, vs], pad], axis=0)
        rows = q_ref[:, g * kv_heads_dev : (g + 1) * kv_heads_dev].astype(BF)
        rows = rows.reshape(4 * kv_heads_dev * tile, HD)
        scores = lax.dot_general(
            rows, keys, (((1,), (1,)), ((), ())), preferred_element_type=F32
        ) * SCALE
        cols = scores.shape[1]
        bias = bias_ref[...].reshape(4, 1, tile, cols)
        masked = jnp.where(bias < 0, LOW, scores.reshape(4, kv_heads_dev, tile, cols))
        masked = masked.reshape(scores.shape)
        top = jnp.max(masked, axis=1, keepdims=True)
        weights = jnp.exp(masked - top)
        total = jnp.sum(weights, axis=1, keepdims=True)
        out = jnp.dot(weights.astype(BF), values, preferred_element_type=F32) / total
        out = out.astype(tdt).reshape(4, kv_heads_dev, tile, HD)
        lane = lax.broadcasted_iota(jnp.int32, (rows.shape[0], HD), 1)
        st = jnp.where(lane == 0, top, jnp.where(lane == 1, total, 0.0))
        st = st.reshape(4, kv_heads_dev, tile, HD)
        for hq in range(kv_heads_dev):
            j = g * kv_heads_dev + hq
            obuf[j, :, nd] = out[:, hq]
            block = st[:, hq].reshape(4 * tile, HD)
            block = jnp.concatenate([block, jnp.zeros((HD - 4 * tile, HD), F32)], axis=0)
            stat[j, 8:16] = block.T[0:8]

    for step in range(nb):
        for part in range(2):
            q_copy(part, step).wait()
            if step + 1 < nb:
                q_copy(part, step + 1).start()

    def peer_copies(j):
        return (
            pltpu.make_async_remote_copy(
                src_ref=obuf.at[j], dst_ref=orecv.at[me], send_sem=o_s.at[j], recv_sem=o_r.at[me],
                device_id={"decode": j}, device_id_type=MESH),
            pltpu.make_async_remote_copy(
                src_ref=stat.at[j], dst_ref=strecv.at[me], send_sem=t_s.at[j], recv_sem=t_r.at[me],
                device_id={"decode": j}, device_id_type=MESH),
        )

    def from_peer(j):
        return (
            pltpu.make_async_remote_copy(
                src_ref=obuf.at[j], dst_ref=orecv.at[j], send_sem=o_s.at[j], recv_sem=o_r.at[j],
                device_id={"decode": j}, device_id_type=MESH),
            pltpu.make_async_remote_copy(
                src_ref=stat.at[j], dst_ref=strecv.at[j], send_sem=t_s.at[j], recv_sem=t_r.at[j],
                device_id={"decode": j}, device_id_type=MESH),
        )

    loads[1].wait()
    m_rows = nd * kv_heads_dev * tile
    for g in range(KVH):
        lane = lax.broadcasted_iota(jnp.int32, (m_rows, HD), 1)
        st = jnp.zeros((m_rows, HD), F32)
        for p in range(4):
            keys = kv[p, :, g * HD : (g + 1) * HD]
            values = kv[p, :, (KVH + g) * HD : (KVH + g + 1) * HD]
            q_at = (p // 2,) + (slice(None),) * nb + (p % 2, slice(g * kv_heads_dev, (g + 1) * kv_heads_dev))
            rows = qall[q_at].astype(BF).reshape(m_rows, HD)
            scores = lax.dot_general(
                rows, keys, (((1,), (1,)), ((), ())), preferred_element_type=F32
            ) * SCALE
            top = jnp.max(scores, axis=1, keepdims=True)
            weights = jnp.exp(scores - top)
            total = jnp.sum(weights, axis=1, keepdims=True)
            out = jnp.dot(weights.astype(BF), values, preferred_element_type=F32) / total
            out = out.astype(tdt).reshape(nd, kv_heads_dev, tile, HD)
            for hq in range(kv_heads_dev):
                obuf[g * kv_heads_dev + hq, p, 0:nd] = out[:, hq]
            st = jnp.where(lane == 2 * p, top, jnp.where(lane == 2 * p + 1, total, st))
        st = st.reshape(nd, kv_heads_dev, tile, HD)
        for hq in range(kv_heads_dev):
            stat[g * kv_heads_dev + hq, 0:8] = st[:, hq].reshape(nd * tile, HD).T[0:8]
        for hq in range(kv_heads_dev):
            j = g * kv_heads_dev + hq

            @pl.when(j != me)
            def _():
                for copy in peer_copies(j):
                    copy.start()

            @pl.when(j == me)
            def _():
                orecv[me] = obuf[me]
                strecv[me] = stat[me]

    for j in range(nd):

        @pl.when(j != me)
        def _():
            for copy in from_peer(j):
                copy.wait()

    turned = strecv[...].reshape(nd * 16, HD).T
    merged = []
    for p in range(4):
        tops = [turned[:, b * 16 + 2 * p : b * 16 + 2 * p + 1] for b in range(nd)]
        sums = [turned[:, b * 16 + 2 * p + 1 : b * 16 + 2 * p + 2] for b in range(nd)]
        span = slice(p * tile, (p + 1) * tile)
        tops.append(jnp.concatenate([turned[span, d * 16 + 8 : d * 16 + 9] for d in range(nd)], axis=0))
        sums.append(jnp.concatenate([turned[span, d * 16 + 9 : d * 16 + 10] for d in range(nd)], axis=0))
        best = functools.reduce(jnp.maximum, tops)
        whole = jnp.zeros_like(best)
        joined = jnp.zeros((nd * tile, HD), F32)
        for b in range(nd + 1):
            factor = jnp.exp(tops[b] - best) * sums[b]
            if b < nd:
                piece = orecv[b, p, 0:nd].reshape(nd * tile, HD)
            else:
                piece = jnp.concatenate([orecv[d, p, nd] for d in range(nd)], axis=0)
            whole = whole + factor
            joined = joined + factor * piece.astype(F32)
        merged.append((joined / whole).astype(BF))
    merged = jnp.concatenate(merged, axis=0)
    row = lax.broadcasted_iota(jnp.int32, (nd * 16, 4 * nd * tile), 0)
    col = lax.broadcasted_iota(jnp.int32, (nd * 16, 4 * nd * tile), 1)
    at = (row // 4) % 4 * (nd * tile) + row // 16 * tile + row % 4
    picked = []
    for h in range(hpd):
        select = jnp.where(col == at + h * 4, 1.0, 0.0).astype(BF)
        picked.append(jnp.dot(select, merged, preferred_element_type=F32).astype(BF))
    attention = jnp.concatenate(picked, axis=1)

    loads[2].wait()
    width = wo.shape[1]
    half = width // 2
    cube = (2,) * nb
    for c in range(0, width, 512):
        part_sum = jnp.dot(attention, wo[:, c : c + 512], preferred_element_type=F32)
        acc[(slice(None),) * (nb + 1) + (slice(c, c + 512),)] = part_sum.astype(BF).reshape(cube + (16, 512))
    s_orders = [dims[-1:] + dims[:-1][::-1], dims[-1:] + dims[:-1]]

    def p_copy(part, step):
        tail = (slice(None), slice(part * half, (part + 1) * half))
        return scatter_copy(
            acc, lands[part][step], dims, s_orders[part], step, tail,
            p_s.at[part, step], p_r.at[part, step],
        )

    for part in range(2):
        p_copy(part, 0).start()
    for step in range(nb):
        for part in range(2):
            p_copy(part, step).wait()
            span = slice(part * half, (part + 1) * half)
            at = cube_index(dims, set(s_orders[part][: step + 1])) + (slice(None), span)
            summed = acc[at].astype(F32) + lands[part][step][...].astype(F32)
            if step + 1 < nb:
                acc[at] = summed.astype(BF)
                p_copy(part, step + 1).start()
            else:
                res_ref[:, span] = hid_ref[:, span].astype(F32) + summed
    residual = res_ref[...]
    scale = lax.rsqrt(jnp.mean(residual * residual, axis=1, keepdims=True) + 1e-06)
    pay_ref[:, 0:width] = (residual * scale * gain_ref[...]).astype(BF)
    pay_ref[:, width:] = gates_ref[...]


def expert_kernel(
    np_, nd, lead, pay_ref, res_ref, wg_ref, wu_ref, wd_ref, out_ref, xbuf, wg, wu, wd, *rest
):
    bp, bd = nbits(np_), nbits(nd)
    nb = bp + bd
    lands = [rest[:nb], rest[nb : 2 * nb]]
    local_sem, g_s, g_r, p_s, p_r = rest[2 * nb :]
    prompt = [("prompt", k) for k in range(bp - 1, -1, -1)]
    decode = [("decode", k) for k in range(bd - 1, -1, -1)]
    dims = prompt + decode
    orders = [prompt + decode, prompt + decode[:-1][::-1] + decode[-1:]]
    width = res_ref.shape[1]
    full = pay_ref.shape[1]
    loads = [
        pltpu.make_async_copy(wg_ref, wg, local_sem.at[0]),
        pltpu.make_async_copy(wu_ref, wu, local_sem.at[1]),
        pltpu.make_async_copy(wd_ref, wd, local_sem.at[2]),
    ]
    for load in loads:
        load.start()
    barrier = pltpu.get_barrier_semaphore()
    for dim in dims:
        pl.semaphore_signal(barrier, inc=1, device_id=partner(*dim), device_id_type=MESH)
    xbuf[cube_index(dims, set(dims))] = pay_ref[...]
    pl.semaphore_wait(barrier, nb)

    def g_copy(part, step):
        tail = (slice(None), slice(part * full // 2, (part + 1) * full // 2))
        return gather_copy(xbuf, dims, orders[part], step, tail, g_s.at[part, step], g_r.at[part, step])

    for part in range(2):
        g_copy(part, 0).start()
    for step in range(nb):
        for part in range(2):
            g_copy(part, step).wait()
            if step + 1 < nb:
                g_copy(part, step + 1).start()
    for load in loads:
        load.wait()

    expert = lax.axis_index("prompt") * nd + lax.axis_index("decode")
    rest_dims = (2,) * (nb - lead)
    m = 16 * 2 ** (nb - lead)

    def block(i, carry):
        at = tuple((i // (1 << (lead - 1 - k))) % 2 for k in range(lead))
        at = at + (slice(None),) * (nb - lead + 1)
        x = xbuf[at + (slice(0, width),)].reshape(m, width)
        gates = xbuf[at + (slice(width, full),)].reshape(m, full - width).astype(F32)
        both = gates[:, 0 : (full - width) // 2] + gates[:, (full - width) // 2 :]
        lane = lax.broadcasted_iota(jnp.int32, both.shape, 1)
        gate = jnp.sum(jnp.where(lane == expert, both, 0.0), axis=1, keepdims=True)
        gated = jnp.dot(x, wg[...], preferred_element_type=F32)
        lifted = jnp.dot(x, wu[...], preferred_element_type=F32)
        act = (gated / (1.0 + jnp.exp(-gated)) * lifted).astype(BF)
        for c in range(0, width, 1024):
            y = jnp.dot(act, wd[:, c : c + 1024], preferred_element_type=F32)
            y = jnp.where(gate > 0, gate * y, 0.0).astype(BF)
            xbuf[at + (slice(c, c + 1024),)] = y.reshape(rest_dims + (16, 1024))
        return carry

    lax.fori_loop(0, 1 << lead, block, 0)

    half = width // 2

    def p_copy(part, step):
        tail = (slice(None), slice(part * half, (part + 1) * half))
        return scatter_copy(
            xbuf, lands[part][step], dims, orders[part][::-1], step, tail,
            p_s.at[part, step], p_r.at[part, step],
        )

    for part in range(2):
        p_copy(part, 0).start()
    for step in range(nb):
        for part in range(2):
            p_copy(part, step).wait()
            span = slice(part * half, (part + 1) * half)
            at = cube_index(dims, set(orders[part][::-1][: step + 1])) + (slice(None), span)
            summed = xbuf[at].astype(F32) + lands[part][step][...].astype(F32)
            if step + 1 < nb:
                xbuf[at] = summed.astype(BF)
                p_copy(part, step + 1).start()
            else:
                out_ref[:, span] = (res_ref[:, span] + summed).astype(BF)


def per_device(
    np_, nd, hidden_in, queries, new_kv, prompt_kv, sample_kv, counts, out_proj, norm_gain,
    expert_ids, expert_gates, w_gate, w_up, w_down,
):
    prompts, samples, width = hidden_in.shape
    rows = prompts * samples
    hpd = out_proj.shape[0] // HD
    tile = hpd * samples
    groups = H // hpd
    tdt = BF if tile % 16 == 0 else F32
    gen = sample_kv.shape[2]
    experts = np_ * nd
    vmem = pl.BlockSpec(memory_space=pltpu.VMEM)
    hbm = pl.BlockSpec(memory_space=pl.ANY)

    q = queries.reshape(prompts, samples, groups, hpd, HD).transpose(0, 2, 3, 1, 4)
    q = q.reshape(prompts, groups, tile, HD).astype(tdt)
    cols = rows * gen + 128
    col = jnp.arange(cols, dtype=jnp.int32)[None, :]
    row = jnp.arange(rows, dtype=jnp.int32)[:, None]
    own = (col // gen == row) & (col % gen < counts.reshape(rows, 1))
    valid = jnp.where(col < rows * gen, own, col - rows * gen == row)
    bias = jnp.where(valid, 0.0, -1.0).astype(F32).reshape(prompts, 1, samples, cols)
    bias = jnp.broadcast_to(bias, (prompts, hpd, samples, cols)).reshape(prompts, tile, cols)
    hot = expert_ids.reshape(rows, TOPK, 1) == jnp.arange(128, dtype=jnp.int32)
    gates = jnp.sum(jnp.where(hot, expert_gates.reshape(rows, TOPK, 1), 0.0), axis=1)
    high = lax.reduce_precision(gates, 8, 7)
    gates = jnp.concatenate([high, gates - high], axis=1).astype(BF)

    nb = nbits(nd)
    half = width // 2
    cube = (2,) * nb
    dma = pltpu.SemaphoreType.DMA
    lands = [pltpu.VMEM((2,) * (nb - 1 - step) + (16, half), BF) for step in range(nb)]
    residual, payload = pl.pallas_call(
        functools.partial(attention_kernel, nd, hpd, tdt),
        out_shape=(
            jax.ShapeDtypeStruct((rows, width), F32),
            jax.ShapeDtypeStruct((rows, width + 256), BF),
        ),
        in_specs=[vmem, hbm, hbm, vmem, vmem, hbm, vmem, vmem, vmem],
        out_specs=(vmem, vmem),
        scratch_shapes=[
            pltpu.VMEM((2,) + cube + (2, groups, tile, HD), tdt),
            pltpu.VMEM(prompt_kv.shape, BF),
            pltpu.VMEM((rows * gen, sample_kv.shape[3]), BF),
            pltpu.VMEM(out_proj.shape, BF),
            pltpu.VMEM((nd, prompts, nd + 1, tile, HD), tdt),
            pltpu.VMEM((nd, prompts, nd + 1, tile, HD), tdt),
            pltpu.VMEM((nd, 16, HD), F32),
            pltpu.VMEM((nd, 16, HD), F32),
            pltpu.VMEM(cube + (16, width), BF),
        ]
        + lands
        + lands
        + [dma((3,)), dma((2, nb)), dma((2, nb)), dma((nd,)), dma((nd,)), dma((nd,)), dma((nd,)),
           dma((2, nb)), dma((2, nb))],
        compiler_params=pltpu.CompilerParams(
            collective_id=0, has_side_effects=True, vmem_limit_bytes=48 * 2**20
        ),
        name="attention",
    )(
        q, prompt_kv, sample_kv.reshape(rows * gen, sample_kv.shape[3]),
        new_kv.reshape(rows, new_kv.shape[2]), bias, out_proj, hidden_in.reshape(rows, width),
        norm_gain.reshape(1, width), gates,
    )

    nb = nbits(np_) + nbits(nd)
    lands = [pltpu.VMEM((2,) * (nb - 1 - step) + (16, half), BF) for step in range(nb)]
    mixed = pl.pallas_call(
        functools.partial(expert_kernel, np_, nd, max(0, nb - 4)),
        out_shape=jax.ShapeDtypeStruct((rows, width), BF),
        in_specs=[vmem, vmem, hbm, hbm, hbm],
        out_specs=vmem,
        scratch_shapes=[
            pltpu.VMEM((2,) * nb + (16, width + 256), BF),
            pltpu.VMEM(w_gate.shape[1:], BF),
            pltpu.VMEM(w_up.shape[1:], BF),
            pltpu.VMEM(w_down.shape[1:], BF),
        ]
        + lands
        + lands
        + [dma((3,)), dma((2, nb)), dma((2, nb)), dma((2, nb)), dma((2, nb))],
        compiler_params=pltpu.CompilerParams(
            collective_id=1, has_side_effects=True, vmem_limit_bytes=62 * 2**20
        ),
        name="experts",
    )(payload, residual, w_gate[0], w_up[0], w_down[0])
    return mixed.reshape(prompts, samples, width)


def solution(mesh):
    in_specs = (
        P("prompt", "decode", None),
        P("prompt", "decode", None),
        P("prompt", "decode", None),
        P("prompt", "decode", None),
        P("prompt", "decode", None, None),
        P("prompt", "decode"),
        P("decode", None),
        P(),
        P("prompt", "decode", None, None),
        P("prompt", "decode", None, None),
        P(("prompt", "decode"), None, None),
        P(("prompt", "decode"), None, None),
        P(("prompt", "decode"), None, None),
    )
    return jax.shard_map(
        functools.partial(per_device, mesh.shape["prompt"], mesh.shape["decode"]),
        mesh=mesh, in_specs=in_specs, out_specs=P("prompt", "decode", None), check_vma=False,
    )
```

```python
import functools

import jax
import jax.numpy as jnp
from jax import lax
from jax.experimental import pallas as pl
from jax.experimental.pallas import tpu as pltpu
from jax.sharding import PartitionSpec as P

H = 32
KVH = 2
HD = 128
TOPK = 8
GROUPS = H // KVH
SCALE = HD ** (-0.5)
LOW = -1e30
MESH = pl.DeviceIdType.MESH
BF = jnp.bfloat16
F32 = jnp.float32


def nbits(n):
    return n.bit_length() - 1


def bit_of(axis, k):
    return lax.rem(lax.axis_index(axis) // (1 << k), 2)


def partner(axis, k):
    me = lax.axis_index(axis)
    return {axis: me + (1 - 2 * bit_of(axis, k)) * (1 << k)}


def cube_index(dims, fixed, flip=None):
    out = []
    for dim in dims:
        if dim == flip:
            out.append(1 - bit_of(*dim))
        elif dim in fixed:
            out.append(bit_of(*dim))
        else:
            out.append(slice(None))
    return tuple(out)


def gather_copy(ref, dims, order, step, tail, ssem, rsem):
    fixed = set(order[step:])
    view = ref.at[cube_index(dims, fixed) + tail]
    return pltpu.make_async_remote_copy(
        src_ref=view, dst_ref=view, send_sem=ssem, recv_sem=rsem,
        device_id=partner(*order[step]), device_id_type=MESH,
    )


def scatter_copy(ref, land, dims, order, step, tail, ssem, rsem):
    fixed = set(order[:step])
    view = ref.at[cube_index(dims, fixed, flip=order[step]) + tail]
    return pltpu.make_async_remote_copy(
        src_ref=view, dst_ref=land, send_sem=ssem, recv_sem=rsem,
        device_id=partner(*order[step]), device_id_type=MESH,
    )


def attention_kernel(
    nd, hpd, tdt,
    q_ref, kv_ref, skv_ref, nkv_ref, counts_ref, wo_ref, hid_ref, gain_ref, ids_ref, gates_ref,
    res_ref, pay_ref,
    qown, qall, kv, skv, wo, obuf, orecv, stat, strecv, acc, *rest,
):
    nb = nbits(nd)
    lands = [rest[:nb], rest[nb : 2 * nb]]
    local_sem, q_s, q_r, o_s, o_r, t_s, t_r, p_s, p_r = rest[2 * nb :]
    me = lax.axis_index("decode")
    dims = [("decode", k) for k in range(nb - 1, -1, -1)]
    orders = [dims[:-1][::-1] + dims[-1:], dims[:-1] + dims[-1:]]
    tile = hpd * 4
    kv_heads_dev = GROUPS // hpd

    loads = [
        pltpu.make_async_copy(skv_ref, skv, local_sem.at[0]),
        pltpu.make_async_copy(kv_ref, kv, local_sem.at[1]),
        pltpu.make_async_copy(wo_ref, wo, local_sem.at[2]),
    ]
    for load in loads:
        load.start()

    barrier = pltpu.get_barrier_semaphore()
    for k in range(1, nd):
        pl.semaphore_signal(
            barrier, inc=1, device_id={"decode": lax.rem(me + k, nd)}, device_id_type=MESH
        )
    mine = cube_index(dims, set(dims))
    for p in range(4):
        row = q_ref[p].astype(F32)
        for hq in range(H // hpd):
            heads = [row[:, h * HD : (h + 1) * HD] for h in range(hq * hpd, (hq + 1) * hpd)]
            qown[p, hq] = jnp.concatenate(heads, axis=0).astype(tdt)
    for part in range(2):
        qall[(part,) + mine] = qown[2 * part : 2 * part + 2]
    pl.semaphore_wait(barrier, nd - 1)

    def q_copy(part, step):
        return gather_copy(
            qall.at[part], dims, orders[part], step, (), q_s.at[part, step], q_r.at[part, step]
        )

    for part in range(2):
        q_copy(part, 0).start()

    loads[0].wait()
    gen = skv.shape[2]
    cached = 16 * gen
    fresh = jnp.concatenate([nkv_ref[p].astype(F32) for p in range(4)], axis=0).astype(BF)
    col = lax.broadcasted_iota(jnp.int32, (tile, cached + 128), 1)
    sample = lax.rem(lax.broadcasted_iota(jnp.int32, (tile, cached + 128), 0), 4)
    lane4 = lax.broadcasted_iota(jnp.int32, (tile, 4), 1)
    own4 = lax.rem(lax.broadcasted_iota(jnp.int32, (tile, 4), 0), 4) == lane4
    biases = []
    for p in range(4):
        count = jnp.sum(
            jnp.where(own4, counts_ref[p : p + 1, :].astype(F32), 0.0), axis=1, keepdims=True
        ).astype(jnp.int32)
        first = (sample + 4 * p) * gen
        valid = ((col >= first) & (col < first + count)) | (col == cached + 4 * p + sample)
        biases.append(jnp.where(valid, 0.0, -1.0))
    bias = jnp.concatenate(biases, axis=0).reshape(4, 1, tile, cached + 128)
    for g in range(KVH):
        ks, vs = slice(g * HD, (g + 1) * HD), slice((KVH + g) * HD, (KVH + g + 1) * HD)
        pad = jnp.zeros((112, HD), BF)
        keys = jnp.concatenate([skv[:, :, :, ks].reshape(cached, HD), fresh[:, ks], pad], axis=0)
        values = jnp.concatenate([skv[:, :, :, vs].reshape(cached, HD), fresh[:, vs], pad], axis=0)
        rows = qown[:, g * kv_heads_dev : (g + 1) * kv_heads_dev].astype(BF)
        rows = rows.reshape(4 * kv_heads_dev * tile, HD)
        scores = lax.dot_general(
            rows, keys, (((1,), (1,)), ((), ())), preferred_element_type=F32
        ) * SCALE
        cols = scores.shape[1]
        masked = jnp.where(bias < 0, LOW, scores.reshape(4, kv_heads_dev, tile, cols))
        masked = masked.reshape(scores.shape)
        top = jnp.max(masked, axis=1, keepdims=True)
        weights = jnp.exp(masked - top)
        total = jnp.sum(weights, axis=1, keepdims=True)
        out = jnp.dot(weights.astype(BF), values, preferred_element_type=F32) / total
        out = out.astype(tdt).reshape(4, kv_heads_dev, tile, HD)
        lane = lax.broadcasted_iota(jnp.int32, (rows.shape[0], HD), 1)
        st = jnp.where(lane == 0, top, jnp.where(lane == 1, total, 0.0))
        st = st.reshape(4, kv_heads_dev, tile, HD)
        for hq in range(kv_heads_dev):
            j = g * kv_heads_dev + hq
            obuf[j, :, nd] = out[:, hq]
            block = st[:, hq].reshape(4 * tile, HD)
            block = jnp.concatenate([block, jnp.zeros((HD - 4 * tile, HD), F32)], axis=0)
            stat[j, 8:16] = block.T[0:8]

    for step in range(nb):
        for part in range(2):
            q_copy(part, step).wait()
            if step + 1 < nb:
                q_copy(part, step + 1).start()

    def out_copy(j, p, source):
        return pltpu.make_async_remote_copy(
            src_ref=obuf.at[j, p], dst_ref=orecv.at[source, p],
            send_sem=o_s.at[j, p], recv_sem=o_r.at[source, p],
            device_id={"decode": j}, device_id_type=MESH)

    def stat_copy(j, source):
        return pltpu.make_async_remote_copy(
            src_ref=stat.at[j], dst_ref=strecv.at[source],
            send_sem=t_s.at[j], recv_sem=t_r.at[source],
            device_id={"decode": j}, device_id_type=MESH)

    peers = [lax.rem(me + k, nd) for k in range(1, nd)]
    loads[1].wait()
    m_rows = nd * kv_heads_dev * tile
    lane = lax.broadcasted_iota(jnp.int32, (m_rows, HD), 1)
    stats = [jnp.zeros((m_rows, HD), F32) for _ in range(KVH)]
    for p in range(4):
        for g in range(KVH):
            keys = kv[p, :, g * HD : (g + 1) * HD]
            values = kv[p, :, (KVH + g) * HD : (KVH + g + 1) * HD]
            q_at = (p // 2,) + (slice(None),) * nb + (p % 2, slice(g * kv_heads_dev, (g + 1) * kv_heads_dev))
            rows = qall[q_at].astype(BF).reshape(m_rows, HD)
            scores = lax.dot_general(
                rows, keys, (((1,), (1,)), ((), ())), preferred_element_type=F32
            ) * SCALE
            top = jnp.max(scores, axis=1, keepdims=True)
            weights = jnp.exp(scores - top)
            total = jnp.sum(weights, axis=1, keepdims=True)
            out = jnp.dot(weights.astype(BF), values, preferred_element_type=F32) / total
            out = out.astype(tdt).reshape(nd, kv_heads_dev, tile, HD)
            for hq in range(kv_heads_dev):
                obuf[g * kv_heads_dev + hq, p, 0:nd] = out[:, hq]
            stats[g] = jnp.where(lane == 2 * p, top, jnp.where(lane == 2 * p + 1, total, stats[g]))
        for j in peers:
            out_copy(j, p, me).start()
    for g in range(KVH):
        st = stats[g].reshape(nd, kv_heads_dev, tile, HD)
        for hq in range(kv_heads_dev):
            stat[g * kv_heads_dev + hq, 0:8] = st[:, hq].reshape(nd * tile, HD).T[0:8]
    for j in peers:
        stat_copy(j, me).start()
    orecv[me] = obuf[me]
    strecv[me] = stat[me]
    for j in peers:
        stat_copy(j, j).wait()
    for p in range(4):
        for j in peers:
            out_copy(j, p, j).wait()

    turned = strecv[...].reshape(nd * 16, HD).T
    merged = []
    for p in range(4):
        tops = [turned[:, b * 16 + 2 * p : b * 16 + 2 * p + 1] for b in range(nd)]
        sums = [turned[:, b * 16 + 2 * p + 1 : b * 16 + 2 * p + 2] for b in range(nd)]
        span = slice(p * tile, (p + 1) * tile)
        tops.append(jnp.concatenate([turned[span, d * 16 + 8 : d * 16 + 9] for d in range(nd)], axis=0))
        sums.append(jnp.concatenate([turned[span, d * 16 + 9 : d * 16 + 10] for d in range(nd)], axis=0))
        best = functools.reduce(jnp.maximum, tops)
        whole = jnp.zeros_like(best)
        joined = jnp.zeros((nd * tile, HD), F32)
        for b in range(nd + 1):
            factor = jnp.exp(tops[b] - best) * sums[b]
            if b < nd:
                piece = orecv[b, p, 0:nd].reshape(nd * tile, HD)
            else:
                piece = jnp.concatenate([orecv[d, p, nd] for d in range(nd)], axis=0)
            whole = whole + factor
            joined = joined + factor * piece.astype(F32)
        merged.append((joined / whole).astype(BF))
    merged = jnp.concatenate(merged, axis=0)
    row = lax.broadcasted_iota(jnp.int32, (nd * 16, 4 * nd * tile), 0)
    col = lax.broadcasted_iota(jnp.int32, (nd * 16, 4 * nd * tile), 1)
    at = (row // 4) % 4 * (nd * tile) + row // 16 * tile + row % 4
    picked = []
    for h in range(hpd):
        select = jnp.where(col == at + h * 4, 1.0, 0.0).astype(BF)
        picked.append(jnp.dot(select, merged, preferred_element_type=F32).astype(BF))
    attention = jnp.concatenate(picked, axis=1)

    loads[2].wait()
    width = wo.shape[1]
    half = width // 2
    cube = (2,) * nb
    for c in range(0, width, 512):
        part_sum = jnp.dot(attention, wo[:, c : c + 512], preferred_element_type=F32)
        acc[(slice(None),) * (nb + 1) + (slice(c, c + 512),)] = part_sum.astype(BF).reshape(cube + (16, 512))
    s_orders = [dims[-1:] + dims[:-1][::-1], dims[-1:] + dims[:-1]]

    def p_copy(part, step):
        tail = (slice(None), slice(part * half, (part + 1) * half))
        return scatter_copy(
            acc, lands[part][step], dims, s_orders[part], step, tail,
            p_s.at[part, step], p_r.at[part, step],
        )

    for part in range(2):
        p_copy(part, 0).start()
    for step in range(nb):
        for part in range(2):
            p_copy(part, step).wait()
            span = slice(part * half, (part + 1) * half)
            at = cube_index(dims, set(s_orders[part][: step + 1])) + (slice(None), span)
            summed = acc[at].astype(F32) + lands[part][step][...].astype(F32)
            if step + 1 < nb:
                acc[at] = summed.astype(BF)
                p_copy(part, step + 1).start()
            else:
                hidden = [hid_ref[p, :, span].astype(F32) for p in range(4)]
                res_ref[:, span] = jnp.concatenate(hidden, axis=0) + summed
    residual = res_ref[...]
    scale = lax.rsqrt(jnp.mean(residual * residual, axis=1, keepdims=True) + 1e-06)
    pay_ref[:, 0:width] = (residual * scale * gain_ref[...]).astype(BF)
    ids, gates = ids_ref[0, 0], gates_ref[0, 0]
    lane = lax.broadcasted_iota(jnp.int32, (16, HD), 1)
    table = jnp.zeros((16, HD), F32)
    for k in range(TOPK):
        table = jnp.where(lane == ids[:, k : k + 1], gates[:, k : k + 1], table)
    high = table.astype(BF)
    pay_ref[:, width : width + HD] = high
    pay_ref[:, width + HD :] = (table - high.astype(F32)).astype(BF)


def expert_kernel(
    np_, nd, pay_ref, res_ref, wg_ref, wu_ref, wd_ref, out_ref, xbuf, wg, wu, wd, zland, *rest
):
    nb = nbits(nd)
    lands = [rest[:nb], rest[nb : 2 * nb]]
    local_sem, g_s, g_r, r_s, r_r, z_s, z_r, y_s, y_r = rest[2 * nb :]
    dims = [("decode", k) for k in range(nb - 1, -1, -1)]
    orders = [dims, dims[:-1][::-1] + dims[-1:]]
    mine = cube_index(dims, set(dims))
    width = res_ref.shape[1]
    full = pay_ref.shape[1]
    half = width // 2
    spans = [slice(0, half), slice(half, width)]
    loads = [
        pltpu.make_async_copy(wg_ref.at[0], wg, local_sem.at[0]),
        pltpu.make_async_copy(wu_ref.at[0], wu, local_sem.at[1]),
        pltpu.make_async_copy(wd_ref.at[0], wd, local_sem.at[2]),
    ]
    for load in loads:
        load.start()

    def across(k):
        bits = [bit_of("prompt", b) for b in range(nbits(np_))]
        bits = [1 - bit if (k >> b) % 2 else bit for b, bit in enumerate(bits)]
        return {"prompt": sum(bit * (1 << b) for b, bit in enumerate(bits))}

    barrier = pltpu.get_barrier_semaphore()
    for dim in dims:
        pl.semaphore_signal(barrier, inc=1, device_id=partner(*dim), device_id_type=MESH)
    for k in range(1, np_):
        pl.semaphore_signal(barrier, inc=1, device_id=across(k), device_id_type=MESH)
    xbuf[(0,) + mine] = pay_ref[...]
    pl.semaphore_wait(barrier, nb + np_ - 1)

    def z_in(k):
        return pltpu.make_async_remote_copy(
            src_ref=pay_ref, dst_ref=xbuf.at[(k,) + mine], send_sem=z_s.at[k], recv_sem=z_r.at[k],
            device_id=across(k), device_id_type=MESH)

    def z_out(k):
        return pltpu.make_async_remote_copy(
            src_ref=xbuf.at[(k,) + mine + (slice(None), slice(0, width))], dst_ref=zland.at[k],
            send_sem=y_s.at[k], recv_sem=y_r.at[k], device_id=across(k), device_id_type=MESH)

    def gather(k, part, step):
        tail = (slice(None), slice(part * full // 2, (part + 1) * full // 2))
        return gather_copy(
            xbuf.at[k], dims, orders[part], step, tail, g_s.at[k, part, step], g_r.at[k, part, step]
        )

    def scatter(k, part, step):
        return scatter_copy(
            xbuf.at[k], lands[part][step].at[k], dims, orders[part][::-1], step,
            (slice(None), spans[part]), r_s.at[k, part, step], r_r.at[k, part, step],
        )

    expert = lax.axis_index("prompt") * nd + lax.axis_index("decode")
    m = nd * 16
    cube = (2,) * nb

    def compute(k):
        at = (k,) + (slice(None),) * (nb + 1)
        x = xbuf[at + (slice(0, width),)].reshape(m, width)
        gates = xbuf[at + (slice(width, full),)].reshape(m, full - width).astype(F32)
        both = gates[:, 0:HD] + gates[:, HD:]
        lane = lax.broadcasted_iota(jnp.int32, both.shape, 1)
        gate = jnp.sum(jnp.where(lane == expert, both, 0.0), axis=1, keepdims=True)
        gated = jnp.dot(x, wg[...], preferred_element_type=F32)
        lifted = jnp.dot(x, wu[...], preferred_element_type=F32)
        act = (gated / (1.0 + jnp.exp(-gated)) * lifted).astype(BF)
        for c in range(0, width, 1024):
            y = jnp.dot(act, wd[:, c : c + 1024], preferred_element_type=F32)
            y = jnp.where(gate > 0, gate * y, 0.0).astype(BF)
            xbuf[at + (slice(c, c + 1024),)] = y.reshape(cube + (16, 1024))

    def reduce(k, step):
        for part in range(2):
            scatter(k, part, step - 1).wait()
            at = (k,) + cube_index(dims, set(orders[part][::-1][:step])) + (slice(None), spans[part])
            summed = xbuf[at].astype(F32) + lands[part][step - 1][k].astype(F32)
            if step == nb and k == 0:
                res_ref_sum = res_ref[:, spans[part]] + summed
                for other in range(1, np_):
                    if part == 0:
                        z_out(other).wait()
                    res_ref_sum = res_ref_sum + zland[other, :, spans[part]].astype(F32)
                for p in range(4):
                    out_ref[p, :, spans[part]] = res_ref_sum[4 * p : 4 * p + 4].astype(BF)
            else:
                xbuf[at] = summed.astype(BF)
                if step < nb:
                    scatter(k, part, step).start()
        if step == nb and k > 0:
            z_out(k).start()

    for k in range(1, np_):
        z_in(k).start()
    for tick in range(1 + 2 * nb + np_):
        for k in range(np_):
            step = tick - k
            if 0 <= step <= nb:
                if step == 0 and k > 0:
                    z_in(k).wait()
                for part in range(2):
                    if step > 0:
                        gather(k, part, step - 1).wait()
                    if step < nb:
                        gather(k, part, step).start()
        now = tick - 1 - nb
        if 0 <= now < np_:
            if now == 0:
                for load in loads:
                    load.wait()
            compute((now + 1) % np_)
            for part in range(2):
                scatter((now + 1) % np_, part, 0).start()
        for turn in range(np_):
            step = now - turn
            if 1 <= step <= nb:
                reduce((turn + 1) % np_, step)


def per_device(
    np_, nd, hidden_in, queries, new_kv, prompt_kv, sample_kv, counts, out_proj, norm_gain,
    expert_ids, expert_gates, w_gate, w_up, w_down,
):
    prompts, samples, width = hidden_in.shape
    rows = prompts * samples
    hpd = out_proj.shape[0] // HD
    tile = hpd * samples
    groups = H // hpd
    tdt = BF if tile % 16 == 0 else F32
    vmem = pl.BlockSpec(memory_space=pltpu.VMEM)
    hbm = pl.BlockSpec(memory_space=pl.ANY)

    nb = nbits(nd)
    half = width // 2
    cube = (2,) * nb
    dma = pltpu.SemaphoreType.DMA
    lands = [pltpu.VMEM((2,) * (nb - 1 - step) + (16, half), BF) for step in range(nb)]
    residual, payload = pl.pallas_call(
        functools.partial(attention_kernel, nd, hpd, tdt),
        out_shape=(
            jax.ShapeDtypeStruct((rows, width), F32),
            jax.ShapeDtypeStruct((rows, width + 256), BF),
        ),
        in_specs=[vmem, hbm, hbm, vmem, vmem, hbm, vmem, vmem, vmem, vmem],
        out_specs=(vmem, vmem),
        scratch_shapes=[
            pltpu.VMEM((prompts, groups, tile, HD), tdt),
            pltpu.VMEM((2,) + cube + (2, groups, tile, HD), tdt),
            pltpu.VMEM(prompt_kv.shape, BF),
            pltpu.VMEM(sample_kv.shape, BF),
            pltpu.VMEM(out_proj.shape, BF),
            pltpu.VMEM((nd, prompts, nd + 1, tile, HD), tdt),
            pltpu.VMEM((nd, prompts, nd + 1, tile, HD), tdt),
            pltpu.VMEM((nd, 16, HD), F32),
            pltpu.VMEM((nd, 16, HD), F32),
            pltpu.VMEM(cube + (16, width), BF),
        ]
        + lands
        + lands
        + [dma((3,)), dma((2, nb)), dma((2, nb)), dma((nd, 4)), dma((nd, 4)), dma((nd,)), dma((nd,)),
           dma((2, nb)), dma((2, nb))],
        compiler_params=pltpu.CompilerParams(
            collective_id=0, has_side_effects=True, vmem_limit_bytes=48 * 2**20
        ),
        name="attention",
    )(
        queries, prompt_kv, sample_kv, new_kv, counts, out_proj, hidden_in,
        norm_gain.reshape(1, width), expert_ids, expert_gates,
    )

    lands = [pltpu.VMEM((np_,) + (2,) * (nb - 1 - step) + (16, half), BF) for step in range(nb)]
    return pl.pallas_call(
        functools.partial(expert_kernel, np_, nd),
        out_shape=jax.ShapeDtypeStruct(hidden_in.shape, BF),
        in_specs=[vmem, vmem, hbm, hbm, hbm],
        out_specs=vmem,
        scratch_shapes=[
            pltpu.VMEM((np_,) + cube + (16, width + 256), BF),
            pltpu.VMEM(w_gate.shape[1:], BF),
            pltpu.VMEM(w_up.shape[1:], BF),
            pltpu.VMEM(w_down.shape[1:], BF),
            pltpu.VMEM((np_, rows, width), BF),
        ]
        + lands
        + lands
        + [dma((3,))] + [dma((np_, 2, nb)) for _ in range(4)] + [dma((np_,)) for _ in range(4)],
        compiler_params=pltpu.CompilerParams(
            collective_id=1, has_side_effects=True, vmem_limit_bytes=62 * 2**20
        ),
        name="experts",
    )(payload, residual, w_gate, w_up, w_down)


def solution(mesh):
    in_specs = (
        P("prompt", "decode", None),
        P("prompt", "decode", None),
        P("prompt", "decode", None),
        P("prompt", "decode", None),
        P("prompt", "decode", None, None),
        P("prompt", "decode"),
        P("decode", None),
        P(),
        P("prompt", "decode", None, None),
        P("prompt", "decode", None, None),
        P(("prompt", "decode"), None, None),
        P(("prompt", "decode"), None, None),
        P(("prompt", "decode"), None, None),
    )
    return jax.shard_map(
        functools.partial(per_device, mesh.shape["prompt"], mesh.shape["decode"]),
        mesh=mesh, in_specs=in_specs, out_specs=P("prompt", "decode", None), check_vma=False,
    )
```

```python
import functools

import jax
import jax.numpy as jnp
from jax import lax
from jax.experimental import pallas as pl
from jax.experimental.pallas import tpu as pltpu
from jax.sharding import PartitionSpec as P

H = 32
KVH = 2
HD = 128
TOPK = 8
GROUPS = H // KVH
SCALE = HD ** (-0.5)
LOW = -1e30
MESH = pl.DeviceIdType.MESH
BF = jnp.bfloat16
F32 = jnp.float32


def nbits(n):
    return n.bit_length() - 1


def bit_of(axis, k):
    return lax.rem(lax.axis_index(axis) // (1 << k), 2)


def partner(axis, k):
    me = lax.axis_index(axis)
    return {axis: me + (1 - 2 * bit_of(axis, k)) * (1 << k)}


def cube_index(dims, fixed, flip=None):
    out = []
    for dim in dims:
        if dim == flip:
            out.append(1 - bit_of(*dim))
        elif dim in fixed:
            out.append(bit_of(*dim))
        else:
            out.append(slice(None))
    return tuple(out)


def gather_copy(ref, dims, order, step, tail, ssem, rsem):
    fixed = set(order[step:])
    view = ref.at[cube_index(dims, fixed) + tail]
    return pltpu.make_async_remote_copy(
        src_ref=view, dst_ref=view, send_sem=ssem, recv_sem=rsem,
        device_id=partner(*order[step]), device_id_type=MESH,
    )


def scatter_copy(ref, land, dims, order, step, tail, ssem, rsem):
    fixed = set(order[:step])
    view = ref.at[cube_index(dims, fixed, flip=order[step]) + tail]
    return pltpu.make_async_remote_copy(
        src_ref=view, dst_ref=land, send_sem=ssem, recv_sem=rsem,
        device_id=partner(*order[step]), device_id_type=MESH,
    )


def attention_kernel(
    nd, hpd, tdt,
    q_hbm, kv_ref, skv_ref, nkv_hbm, counts_ref, wo_ref, hid_hbm, gain_ref, ids_ref, gates_ref,
    res_ref, pay_ref,
    q_ref, nkv_ref, hid_ref, qown, qall, kv, skv, wo, obuf, orecv, sbuf, srecv,
    stat, strecv, sstat, ssrecv, acc, *rest,
):
    nb = nbits(nd)
    lands = [rest[:nb], rest[nb : 2 * nb]]
    local_sem, q_s, q_r, k_s, k_r, o_s, o_r, t_s, t_r, d_s, d_r, e_s, e_r, p_s, p_r = rest[2 * nb :]
    me = lax.axis_index("decode")
    dims = [("decode", k) for k in range(nb - 1, -1, -1)]
    orders = [dims[-1:] + dims[:-1][::-1], dims[-1:] + dims[:-1]]
    tile = hpd * 4
    kvd = GROUPS // hpd
    g_mine = bit_of("decode", 0)
    g_mate = 1 - g_mine
    mate = partner("decode", 0)
    pair = me // 2

    def kv_part(g, which):
        at = pl.ds(pl.multiple_of((g + which * KVH) * HD, HD), HD)
        return kv_ref.at[:, :, at], kv.at[g_mine, :, :, which * HD : (which + 1) * HD]

    def kv_send(which):
        src, dst = kv_part(g_mate, which)
        return pltpu.make_async_remote_copy(
            src_ref=src, dst_ref=dst, send_sem=k_s.at[which], recv_sem=k_r.at[which],
            device_id=mate, device_id_type=MESH)

    loads = [
        pltpu.make_async_copy(q_hbm, q_ref, local_sem.at[0]),
        pltpu.make_async_copy(nkv_hbm, nkv_ref, local_sem.at[1]),
        pltpu.make_async_copy(skv_ref, skv, local_sem.at[2]),
        pltpu.make_async_copy(*kv_part(g_mine, 0), local_sem.at[3]),
        pltpu.make_async_copy(*kv_part(g_mine, 1), local_sem.at[4]),
        pltpu.make_async_copy(wo_ref, wo, local_sem.at[5]),
        pltpu.make_async_copy(hid_hbm, hid_ref, local_sem.at[6]),
    ]
    for load in loads:
        load.start()

    barrier = pltpu.get_barrier_semaphore()
    for k in range(1, nd):
        pl.semaphore_signal(
            barrier, inc=1, device_id={"decode": lax.rem(me + k, nd)}, device_id_type=MESH
        )
    mine = cube_index(dims, set(dims))
    loads[0].wait()
    for p in range(4):
        row = q_ref[p].astype(F32)
        for hq in range(H // hpd):
            heads = [row[:, h * HD : (h + 1) * HD] for h in range(hq * hpd, (hq + 1) * hpd)]
            qown[p, hq] = jnp.concatenate(heads, axis=0).astype(tdt)
    for part in range(2):
        qall[(part,) + mine] = qown[2 * part : 2 * part + 2, pl.ds(g_mine * kvd, kvd)]
    pl.semaphore_wait(barrier, nd - 1)

    def q_copy(part, step):
        if step == 0:
            return pltpu.make_async_remote_copy(
                src_ref=qown.at[2 * part : 2 * part + 2, pl.ds(g_mate * kvd, kvd)],
                dst_ref=qall.at[(part,) + mine], send_sem=q_s.at[part, 0], recv_sem=q_r.at[part, 0],
                device_id=mate, device_id_type=MESH)
        return gather_copy(
            qall.at[part], dims, orders[part], step, (), q_s.at[part, step], q_r.at[part, step]
        )

    for part in range(2):
        q_copy(part, 0).start()
    for which in range(2):
        kv_send(which).start()
    for part in range(2):
        q_copy(part, 0).wait()
        q_copy(part, 1).start()

    loads[1].wait()
    loads[2].wait()
    gen = skv.shape[2]
    cached = 16 * gen
    fresh = jnp.concatenate([nkv_ref[p].astype(F32) for p in range(4)], axis=0).astype(BF)
    col = lax.broadcasted_iota(jnp.int32, (tile, cached + 128), 1)
    sample = lax.rem(lax.broadcasted_iota(jnp.int32, (tile, cached + 128), 0), 4)
    lane4 = lax.broadcasted_iota(jnp.int32, (tile, 4), 1)
    own4 = lax.rem(lax.broadcasted_iota(jnp.int32, (tile, 4), 0), 4) == lane4
    biases = []
    for p in range(4):
        count = jnp.sum(
            jnp.where(own4, counts_ref[p : p + 1, :].astype(F32), 0.0), axis=1, keepdims=True
        ).astype(jnp.int32)
        first = (sample + 4 * p) * gen
        valid = ((col >= first) & (col < first + count)) | (col == cached + 4 * p + sample)
        biases.append(jnp.where(valid, 0.0, -1.0))
    bias = jnp.concatenate(biases, axis=0).reshape(4, 1, tile, cached + 128)
    for g in range(KVH):
        ks, vs = slice(g * HD, (g + 1) * HD), slice((KVH + g) * HD, (KVH + g + 1) * HD)
        pad = jnp.zeros((112, HD), BF)
        keys = jnp.concatenate([skv[:, :, :, ks].reshape(cached, HD), fresh[:, ks], pad], axis=0)
        values = jnp.concatenate([skv[:, :, :, vs].reshape(cached, HD), fresh[:, vs], pad], axis=0)
        rows = qown[:, g * kvd : (g + 1) * kvd].astype(BF)
        rows = rows.reshape(4 * kvd * tile, HD)
        scores = lax.dot_general(
            rows, keys, (((1,), (1,)), ((), ())), preferred_element_type=F32
        ) * SCALE
        cols = scores.shape[1]
        masked = jnp.where(bias < 0, LOW, scores.reshape(4, kvd, tile, cols))
        masked = masked.reshape(scores.shape)
        top = jnp.max(masked, axis=1, keepdims=True)
        weights = jnp.exp(masked - top)
        total = jnp.sum(weights, axis=1, keepdims=True)
        out = jnp.dot(weights.astype(BF), values, preferred_element_type=F32) / total
        out = out.astype(tdt).reshape(4, kvd, tile, HD)
        lane = lax.broadcasted_iota(jnp.int32, (rows.shape[0], HD), 1)
        st = jnp.where(lane == 0, top, jnp.where(lane == 1, total, 0.0))
        st = st.reshape(4, kvd, tile, HD)
        for hq in range(kvd):
            j = g * kvd + hq
            sbuf[j] = out[:, hq]
            block = st[:, hq].reshape(4 * tile, HD)
            block = jnp.concatenate([block, jnp.zeros((HD - 4 * tile, HD), F32)], axis=0)
            sstat[j] = block.T[0:8]

    def own_copy(j, source):
        return (
            pltpu.make_async_remote_copy(
                src_ref=sbuf.at[j], dst_ref=srecv.at[source], send_sem=d_s.at[j],
                recv_sem=d_r.at[source], device_id={"decode": j}, device_id_type=MESH),
            pltpu.make_async_remote_copy(
                src_ref=sstat.at[j], dst_ref=ssrecv.at[source], send_sem=e_s.at[j],
                recv_sem=e_r.at[source], device_id={"decode": j}, device_id_type=MESH),
        )

    for step in range(1, nb):
        for part in range(2):
            q_copy(part, step).wait()
            if step + 1 < nb:
                q_copy(part, step + 1).start()
    peers = [lax.rem(me + k, nd) for k in range(1, nd)]
    for j in peers:
        for copy in own_copy(j, me):
            copy.start()
    srecv[me] = sbuf[me]
    ssrecv[me] = sstat[me]

    g_head = me // kvd

    def out_copy(hq, p, slot):
        return pltpu.make_async_remote_copy(
            src_ref=obuf.at[hq, p], dst_ref=orecv.at[slot, p],
            send_sem=o_s.at[hq, p], recv_sem=o_r.at[slot, p],
            device_id={"decode": g_mine * kvd + hq}, device_id_type=MESH)

    def stat_copy(hq, slot):
        return pltpu.make_async_remote_copy(
            src_ref=stat.at[hq], dst_ref=strecv.at[slot],
            send_sem=t_s.at[hq], recv_sem=t_r.at[slot],
            device_id={"decode": g_mine * kvd + hq}, device_id_type=MESH)

    turns = [lax.rem(pair + 1 + k, kvd) for k in range(kvd)]
    for load in loads[3:5]:
        load.wait()
    for which in range(2):
        kv_send(which).wait()
    m_rows = nd * kvd * tile
    lane = lax.broadcasted_iota(jnp.int32, (m_rows, HD), 1)
    st = jnp.zeros((m_rows, HD), F32)
    positions = 2 * kv.shape[2]
    for p in range(4):
        keys = kv[:, p, :, 0:HD].reshape(positions, HD)
        values = kv[:, p, :, HD : 2 * HD].reshape(positions, HD)
        rows = qall[(p // 2,) + (slice(None),) * nb + (p % 2,)].astype(BF).reshape(m_rows, HD)
        scores = lax.dot_general(
            rows, keys, (((1,), (1,)), ((), ())), preferred_element_type=F32
        ) * SCALE
        top = jnp.max(scores, axis=1, keepdims=True)
        weights = jnp.exp(scores - top)
        total = jnp.sum(weights, axis=1, keepdims=True)
        out = jnp.dot(weights.astype(BF), values, preferred_element_type=F32) / total
        out = out.astype(tdt).reshape(nd, kvd, tile, HD)
        for hq in range(kvd):
            obuf[hq, p] = out[:, hq]
        st = jnp.where(lane == 2 * p, top, jnp.where(lane == 2 * p + 1, total, st))
        for hq in turns:

            @pl.when(g_mine * kvd + hq != me)
            def _():
                out_copy(hq, p, pair).start()

    st = st.reshape(nd, kvd, tile, HD)
    for hq in range(kvd):
        stat[hq] = st[:, hq].reshape(nd * tile, HD).T[0:8]
    for hq in turns:

        @pl.when(g_mine * kvd + hq != me)
        def _():
            stat_copy(hq, pair).start()

        @pl.when(g_mine * kvd + hq == me)
        def _():
            orecv[pair] = obuf[hq]
            strecv[pair] = stat[hq]

    for j in peers:
        for copy in own_copy(j, j):
            copy.wait()
    for slot in range(nd // 2):

        @pl.when(2 * slot + g_head != me)
        def _():
            for p in range(4):
                out_copy(0, p, slot).wait_recv()
            stat_copy(0, slot).wait_recv()

    for hq in range(kvd):

        @pl.when(g_mine * kvd + hq != me)
        def _():
            for p in range(4):
                out_copy(hq, p, pair).wait_send()
            stat_copy(hq, pair).wait_send()

    nc = nd // 2
    turned = jnp.concatenate(
        [strecv[...].reshape(nc * 8, HD), ssrecv[...].reshape(nd * 8, HD), jnp.zeros((nd * 4, HD), F32)],
        axis=0,
    ).T
    merged = []
    for p in range(4):
        tops = [turned[:, b * 8 + 2 * p : b * 8 + 2 * p + 1] for b in range(nc)]
        sums = [turned[:, b * 8 + 2 * p + 1 : b * 8 + 2 * p + 2] for b in range(nc)]
        span = slice(p * tile, (p + 1) * tile)
        ats = [(nc + d) * 8 for d in range(nd)]
        tops.append(jnp.concatenate([turned[span, at : at + 1] for at in ats], axis=0))
        sums.append(jnp.concatenate([turned[span, at + 1 : at + 2] for at in ats], axis=0))
        best = functools.reduce(jnp.maximum, tops)
        whole = jnp.zeros_like(best)
        joined = jnp.zeros((nd * tile, HD), F32)
        for b in range(nc + 1):
            factor = jnp.exp(tops[b] - best) * sums[b]
            if b < nc:
                piece = orecv[b, p].reshape(nd * tile, HD)
            else:
                piece = jnp.concatenate([srecv[d, p] for d in range(nd)], axis=0)
            whole = whole + factor
            joined = joined + factor * piece.astype(F32)
        merged.append((joined / whole).astype(BF))
    merged = jnp.concatenate(merged, axis=0)
    row = lax.broadcasted_iota(jnp.int32, (nd * 16, 4 * nd * tile), 0)
    col = lax.broadcasted_iota(jnp.int32, (nd * 16, 4 * nd * tile), 1)
    at = (row // 4) % 4 * (nd * tile) + row // 16 * tile + row % 4
    picked = []
    for h in range(hpd):
        select = jnp.where(col == at + h * 4, 1.0, 0.0).astype(BF)
        picked.append(jnp.dot(select, merged, preferred_element_type=F32).astype(BF))
    attention = jnp.concatenate(picked, axis=1)

    loads[5].wait()
    loads[6].wait()
    width = wo.shape[1]
    half = width // 2
    cube = (2,) * nb
    for c in range(0, width, 512):
        part_sum = jnp.dot(attention, wo[:, c : c + 512], preferred_element_type=F32)
        acc[(slice(None),) * (nb + 1) + (slice(c, c + 512),)] = part_sum.astype(BF).reshape(cube + (16, 512))
    s_orders = [dims[-1:] + dims[:-1][::-1], dims[-1:] + dims[:-1]]

    def p_copy(part, step):
        tail = (slice(None), slice(part * half, (part + 1) * half))
        return scatter_copy(
            acc, lands[part][step], dims, s_orders[part], step, tail,
            p_s.at[part, step], p_r.at[part, step],
        )

    for part in range(2):
        p_copy(part, 0).start()
    for step in range(nb):
        for part in range(2):
            p_copy(part, step).wait()
            span = slice(part * half, (part + 1) * half)
            at = cube_index(dims, set(s_orders[part][: step + 1])) + (slice(None), span)
            summed = acc[at].astype(F32) + lands[part][step][...].astype(F32)
            if step + 1 < nb:
                acc[at] = summed.astype(BF)
                p_copy(part, step + 1).start()
            else:
                hidden = [hid_ref[p, :, span].astype(F32) for p in range(4)]
                res_ref[:, span] = jnp.concatenate(hidden, axis=0) + summed
    residual = res_ref[...]
    scale = lax.rsqrt(jnp.mean(residual * residual, axis=1, keepdims=True) + 1e-06)
    pay_ref[:, 0:width] = (residual * scale * gain_ref[...]).astype(BF)
    routes = jnp.concatenate([ids_ref[...].astype(F32), gates_ref[...]], axis=0)
    routes = jnp.concatenate([routes, jnp.zeros((16, HD - 16), F32)], axis=1)
    routes = jnp.concatenate([routes, jnp.zeros((HD - 16, HD), F32)], axis=0).T[0:16]
    ids, gates = routes[:, 0:TOPK], routes[:, TOPK : 2 * TOPK]
    lane = lax.broadcasted_iota(jnp.int32, (16, HD), 1).astype(F32)
    table = jnp.zeros((16, HD), F32)
    for k in range(TOPK):
        table = jnp.where(lane == ids[:, k : k + 1], gates[:, k : k + 1], table)
    high = table.astype(BF)
    pay_ref[:, width : width + HD] = high
    pay_ref[:, width + HD :] = (table - high.astype(F32)).astype(BF)


def expert_kernel(
    np_, nd, pay_ref, res_ref, wg_ref, wu_ref, wd_ref, out_ref, xbuf, wg, wu, wd, zland, *rest
):
    nb = nbits(nd)
    lands = [rest[:nb], rest[nb : 2 * nb]]
    local_sem, g_s, g_r, r_s, r_r, z_s, z_r, y_s, y_r = rest[2 * nb :]
    dims = [("decode", k) for k in range(nb - 1, -1, -1)]
    orders = [dims, dims[:-1][::-1] + dims[-1:]]
    mine = cube_index(dims, set(dims))
    width = res_ref.shape[1]
    full = pay_ref.shape[1]
    half = width // 2
    spans = [slice(0, half), slice(half, width)]
    loads = [
        pltpu.make_async_copy(wg_ref.at[0], wg, local_sem.at[0]),
        pltpu.make_async_copy(wu_ref.at[0], wu, local_sem.at[1]),
        pltpu.make_async_copy(wd_ref.at[0], wd, local_sem.at[2]),
    ]
    for load in loads:
        load.start()

    def across(k):
        bits = [bit_of("prompt", b) for b in range(nbits(np_))]
        bits = [1 - bit if (k >> b) % 2 else bit for b, bit in enumerate(bits)]
        return {"prompt": sum(bit * (1 << b) for b, bit in enumerate(bits))}

    barrier = pltpu.get_barrier_semaphore()
    for dim in dims:
        pl.semaphore_signal(barrier, inc=1, device_id=partner(*dim), device_id_type=MESH)
    for k in range(1, np_):
        pl.semaphore_signal(barrier, inc=1, device_id=across(k), device_id_type=MESH)
    xbuf[(0,) + mine] = pay_ref[...]
    pl.semaphore_wait(barrier, nb + np_ - 1)

    def z_in(k):
        return pltpu.make_async_remote_copy(
            src_ref=pay_ref, dst_ref=xbuf.at[(k,) + mine], send_sem=z_s.at[k], recv_sem=z_r.at[k],
            device_id=across(k), device_id_type=MESH)

    def z_out(k):
        return pltpu.make_async_remote_copy(
            src_ref=xbuf.at[(k,) + mine + (slice(None), slice(0, width))], dst_ref=zland.at[k],
            send_sem=y_s.at[k], recv_sem=y_r.at[k], device_id=across(k), device_id_type=MESH)

    def gather(k, part, step):
        tail = (slice(None), slice(part * full // 2, (part + 1) * full // 2))
        return gather_copy(
            xbuf.at[k], dims, orders[part], step, tail, g_s.at[k, part, step], g_r.at[k, part, step]
        )

    def scatter(k, part, step):
        return scatter_copy(
            xbuf.at[k], lands[part][step].at[k], dims, orders[part][::-1], step,
            (slice(None), spans[part]), r_s.at[k, part, step], r_r.at[k, part, step],
        )

    expert = lax.axis_index("prompt") * nd + lax.axis_index("decode")
    m = nd * 16
    cube = (2,) * nb

    def compute(k):
        at = (k,) + (slice(None),) * (nb + 1)
        x = xbuf[at + (slice(0, width),)].reshape(m, width)
        gates = xbuf[at + (slice(width, full),)].reshape(m, full - width).astype(F32)
        both = gates[:, 0:HD] + gates[:, HD:]
        lane = lax.broadcasted_iota(jnp.int32, both.shape, 1)
        gate = jnp.sum(jnp.where(lane == expert, both, 0.0), axis=1, keepdims=True)
        gated = jnp.dot(x, wg[...], preferred_element_type=F32)
        lifted = jnp.dot(x, wu[...], preferred_element_type=F32)
        act = (gated / (1.0 + jnp.exp(-gated)) * lifted).astype(BF)
        for c in range(0, width, 1024):
            y = jnp.dot(act, wd[:, c : c + 1024], preferred_element_type=F32)
            y = jnp.where(gate > 0, gate * y, 0.0).astype(BF)
            xbuf[at + (slice(c, c + 1024),)] = y.reshape(cube + (16, 1024))

    def reduce(k, step):
        for part in range(2):
            scatter(k, part, step - 1).wait()
            at = (k,) + cube_index(dims, set(orders[part][::-1][:step])) + (slice(None), spans[part])
            summed = xbuf[at].astype(F32) + lands[part][step - 1][k].astype(F32)
            if step == nb and k == 0:
                res_ref_sum = res_ref[:, spans[part]] + summed
                for other in range(1, np_):
                    if part == 0:
                        z_out(other).wait()
                    res_ref_sum = res_ref_sum + zland[other, :, spans[part]].astype(F32)
                for p in range(4):
                    out_ref[p, :, spans[part]] = res_ref_sum[4 * p : 4 * p + 4].astype(BF)
            else:
                xbuf[at] = summed.astype(BF)
                if step < nb:
                    scatter(k, part, step).start()
        if step == nb and k > 0:
            z_out(k).start()

    for k in range(1, np_):
        z_in(k).start()
    for tick in range(1 + 2 * nb + np_):
        for k in range(np_):
            step = tick - k
            if 0 <= step <= nb:
                if step == 0 and k > 0:
                    z_in(k).wait()
                for part in range(2):
                    if step > 0:
                        gather(k, part, step - 1).wait()
                    if step < nb:
                        gather(k, part, step).start()
        now = tick - 1 - nb
        if 0 <= now < np_:
            if now == 0:
                for load in loads:
                    load.wait()
            compute((now + 1) % np_)
            for part in range(2):
                scatter((now + 1) % np_, part, 0).start()
        for turn in range(np_):
            step = now - turn
            if 1 <= step <= nb:
                reduce((turn + 1) % np_, step)


def per_device(
    np_, nd, hidden_in, queries, new_kv, prompt_kv, sample_kv, counts, out_proj, norm_gain,
    expert_ids, expert_gates, w_gate, w_up, w_down,
):
    prompts, samples, width = hidden_in.shape
    rows = prompts * samples
    hpd = out_proj.shape[0] // HD
    tile = hpd * samples
    groups = H // hpd
    tdt = BF if tile % 16 == 0 else F32
    vmem = pl.BlockSpec(memory_space=pltpu.VMEM)
    hbm = pl.BlockSpec(memory_space=pl.ANY)

    nb = nbits(nd)
    half = width // 2
    cube = (2,) * nb
    dma = pltpu.SemaphoreType.DMA

    def turn(table):
        return table.transpose(0, 1, 3, 2).reshape(TOPK, rows)

    lands = [pltpu.VMEM((2,) * (nb - 1 - step) + (16, half), BF) for step in range(nb)]
    residual, payload = pl.pallas_call(
        functools.partial(attention_kernel, nd, hpd, tdt),
        out_shape=(
            jax.ShapeDtypeStruct((rows, width), F32),
            jax.ShapeDtypeStruct((rows, width + 256), BF),
        ),
        in_specs=[hbm, hbm, hbm, hbm, vmem, hbm, hbm, vmem, vmem, vmem],
        out_specs=(vmem, vmem),
        scratch_shapes=[
            pltpu.VMEM(queries.shape, BF),
            pltpu.VMEM(new_kv.shape, BF),
            pltpu.VMEM(hidden_in.shape, BF),
            pltpu.VMEM((prompts, groups, tile, HD), tdt),
            pltpu.VMEM((2,) + cube + (2, groups // 2, tile, HD), tdt),
            pltpu.VMEM((2, prompts, prompt_kv.shape[1], 2 * HD), BF),
            pltpu.VMEM(sample_kv.shape, BF),
            pltpu.VMEM(out_proj.shape, BF),
            pltpu.VMEM((nd // 2, prompts, nd, tile, HD), tdt),
            pltpu.VMEM((nd // 2, prompts, nd, tile, HD), tdt),
            pltpu.VMEM((nd, prompts, tile, HD), tdt),
            pltpu.VMEM((nd, prompts, tile, HD), tdt),
            pltpu.VMEM((nd // 2, 8, HD), F32),
            pltpu.VMEM((nd // 2, 8, HD), F32),
            pltpu.VMEM((nd, 8, HD), F32),
            pltpu.VMEM((nd, 8, HD), F32),
            pltpu.VMEM(cube + (16, width), BF),
        ]
        + lands
        + lands
        + [dma((7,)), dma((2, nb)), dma((2, nb)), dma((2,)), dma((2,))]
        + [dma((nd // 2, 4)), dma((nd // 2, 4)), dma((nd // 2,)), dma((nd // 2,))]
        + [dma((nd,)) for _ in range(4)]
        + [dma((2, nb)), dma((2, nb))],
        compiler_params=pltpu.CompilerParams(
            collective_id=0, has_side_effects=True, vmem_limit_bytes=62 * 2**20
        ),
        name="attention",
    )(
        queries, prompt_kv, sample_kv, new_kv, counts, out_proj, hidden_in,
        norm_gain.reshape(1, width), turn(expert_ids), turn(expert_gates),
    )

    lands = [pltpu.VMEM((np_,) + (2,) * (nb - 1 - step) + (16, half), BF) for step in range(nb)]
    return pl.pallas_call(
        functools.partial(expert_kernel, np_, nd),
        out_shape=jax.ShapeDtypeStruct(hidden_in.shape, BF),
        in_specs=[vmem, vmem, hbm, hbm, hbm],
        out_specs=vmem,
        scratch_shapes=[
            pltpu.VMEM((np_,) + cube + (16, width + 256), BF),
            pltpu.VMEM(w_gate.shape[1:], BF),
            pltpu.VMEM(w_up.shape[1:], BF),
            pltpu.VMEM(w_down.shape[1:], BF),
            pltpu.VMEM((np_, rows, width), BF),
        ]
        + lands
        + lands
        + [dma((3,))] + [dma((np_, 2, nb)) for _ in range(4)] + [dma((np_,)) for _ in range(4)],
        compiler_params=pltpu.CompilerParams(
            collective_id=1, has_side_effects=True, vmem_limit_bytes=62 * 2**20
        ),
        name="experts",
    )(payload, residual, w_gate, w_up, w_down)


def solution(mesh):
    in_specs = (
        P("prompt", "decode", None),
        P("prompt", "decode", None),
        P("prompt", "decode", None),
        P("prompt", "decode", None),
        P("prompt", "decode", None, None),
        P("prompt", "decode"),
        P("decode", None),
        P(),
        P("prompt", "decode", None, None),
        P("prompt", "decode", None, None),
        P(("prompt", "decode"), None, None),
        P(("prompt", "decode"), None, None),
        P(("prompt", "decode"), None, None),
    )
    return jax.shard_map(
        functools.partial(per_device, mesh.shape["prompt"], mesh.shape["decode"]),
        mesh=mesh, in_specs=in_specs, out_specs=P("prompt", "decode", None), check_vma=False,
    )
```

```python
import functools

import jax
import jax.numpy as jnp
from jax import lax
from jax.experimental import pallas as pl
from jax.experimental.pallas import tpu as pltpu
from jax.sharding import PartitionSpec as P

H = 32
KVH = 2
HD = 128
TOPK = 8
GROUPS = H // KVH
SCALE = HD ** (-0.5)
LOW = -1e30
MESH = pl.DeviceIdType.MESH
BF = jnp.bfloat16
F32 = jnp.float32


def nbits(n):
    return n.bit_length() - 1


def bit_of(axis, k):
    return lax.rem(lax.axis_index(axis) // (1 << k), 2)


def partner(axis, k):
    me = lax.axis_index(axis)
    return {axis: me + (1 - 2 * bit_of(axis, k)) * (1 << k)}


def cube_index(dims, fixed, flip=None):
    out = []
    for dim in dims:
        if dim == flip:
            out.append(1 - bit_of(*dim))
        elif dim in fixed:
            out.append(bit_of(*dim))
        else:
            out.append(slice(None))
    return tuple(out)


def gather_copy(ref, dims, order, step, tail, ssem, rsem):
    fixed = set(order[step:])
    view = ref.at[cube_index(dims, fixed) + tail]
    return pltpu.make_async_remote_copy(
        src_ref=view, dst_ref=view, send_sem=ssem, recv_sem=rsem,
        device_id=partner(*order[step]), device_id_type=MESH,
    )


def scatter_copy(ref, land, dims, order, step, tail, ssem, rsem):
    fixed = set(order[:step])
    view = ref.at[cube_index(dims, fixed, flip=order[step]) + tail]
    return pltpu.make_async_remote_copy(
        src_ref=view, dst_ref=land, send_sem=ssem, recv_sem=rsem,
        device_id=partner(*order[step]), device_id_type=MESH,
    )


def attention_kernel(
    nd, hpd, tdt,
    q_hbm, kv_ref, skv_ref, nkv_hbm, counts_ref, wo_ref, hid_hbm, gain_ref, ids_ref, gates_ref,
    res_ref, pay_ref,
    q_ref, nkv_ref, hid_ref, qown, qall, kv, skv, wo, obuf, orecv, sbuf, srecv,
    stat, strecv, sstat, ssrecv, acc, *rest,
):
    nb = nbits(nd)
    lands = [rest[:nb], rest[nb : 2 * nb]]
    local_sem, q_s, q_r, k_s, k_r, o_s, o_r, t_s, t_r, d_s, d_r, e_s, e_r, p_s, p_r = rest[2 * nb :]
    me = lax.axis_index("decode")
    dims = [("decode", k) for k in range(nb - 1, -1, -1)]
    orders = [dims[-1:] + dims[:-1][::-1], dims[-1:] + dims[:-1]]
    tile = hpd * 4
    kvd = GROUPS // hpd
    g_mine = bit_of("decode", 0)
    g_mate = 1 - g_mine
    mate = partner("decode", 0)
    pair = me // 2

    def kv_part(g, which):
        at = pl.ds(pl.multiple_of((g + which * KVH) * HD, HD), HD)
        return kv_ref.at[:, :, at], kv.at[g_mine, :, :, which * HD : (which + 1) * HD]

    def kv_send(which):
        src, dst = kv_part(g_mate, which)
        return pltpu.make_async_remote_copy(
            src_ref=src, dst_ref=dst, send_sem=k_s.at[which], recv_sem=k_r.at[which],
            device_id=mate, device_id_type=MESH)

    loads = [
        pltpu.make_async_copy(q_hbm, q_ref, local_sem.at[0]),
        pltpu.make_async_copy(nkv_hbm, nkv_ref, local_sem.at[1]),
        pltpu.make_async_copy(skv_ref, skv, local_sem.at[2]),
        pltpu.make_async_copy(*kv_part(g_mine, 0), local_sem.at[3]),
        pltpu.make_async_copy(*kv_part(g_mine, 1), local_sem.at[4]),
        pltpu.make_async_copy(wo_ref, wo, local_sem.at[5]),
        pltpu.make_async_copy(hid_hbm, hid_ref, local_sem.at[6]),
    ]
    for load in loads:
        load.start()

    barrier = pltpu.get_barrier_semaphore()
    for k in range(1, nd):
        pl.semaphore_signal(
            barrier, inc=1, device_id={"decode": lax.rem(me + k, nd)}, device_id_type=MESH
        )
    mine = cube_index(dims, set(dims))
    loads[0].wait()
    for p in range(4):
        row = q_ref[p].astype(F32)
        for hq in range(H // hpd):
            heads = [row[:, h * HD : (h + 1) * HD] for h in range(hq * hpd, (hq + 1) * hpd)]
            qown[p, hq] = jnp.concatenate(heads, axis=0).astype(tdt)
    for part in range(2):
        qall[(part,) + mine] = qown[2 * part : 2 * part + 2, pl.ds(g_mine * kvd, kvd)]
    pl.semaphore_wait(barrier, nd - 1)

    def q_copy(part, step):
        if step == 0:
            return pltpu.make_async_remote_copy(
                src_ref=qown.at[2 * part : 2 * part + 2, pl.ds(g_mate * kvd, kvd)],
                dst_ref=qall.at[(part,) + mine], send_sem=q_s.at[part, 0], recv_sem=q_r.at[part, 0],
                device_id=mate, device_id_type=MESH)
        return gather_copy(
            qall.at[part], dims, orders[part], step, (), q_s.at[part, step], q_r.at[part, step]
        )

    for part in range(2):
        q_copy(part, 0).start()
    for which in range(2):
        kv_send(which).start()
    for part in range(2):
        q_copy(part, 0).wait()
        q_copy(part, 1).start()

    loads[1].wait()
    loads[2].wait()
    gen = skv.shape[2]
    cached = 16 * gen
    fresh = jnp.concatenate([nkv_ref[p].astype(F32) for p in range(4)], axis=0).astype(BF)
    col = lax.broadcasted_iota(jnp.int32, (tile, cached + 128), 1)
    sample = lax.rem(lax.broadcasted_iota(jnp.int32, (tile, cached + 128), 0), 4)
    lane4 = lax.broadcasted_iota(jnp.int32, (tile, 4), 1)
    own4 = lax.rem(lax.broadcasted_iota(jnp.int32, (tile, 4), 0), 4) == lane4
    biases = []
    for p in range(4):
        count = jnp.sum(
            jnp.where(own4, counts_ref[p : p + 1, :].astype(F32), 0.0), axis=1, keepdims=True
        ).astype(jnp.int32)
        first = (sample + 4 * p) * gen
        valid = ((col >= first) & (col < first + count)) | (col == cached + 4 * p + sample)
        biases.append(jnp.where(valid, 0.0, -1.0))
    bias = jnp.concatenate(biases, axis=0).reshape(4, 1, tile, cached + 128)
    for g in range(KVH):
        ks, vs = slice(g * HD, (g + 1) * HD), slice((KVH + g) * HD, (KVH + g + 1) * HD)
        pad = jnp.zeros((112, HD), BF)
        keys = jnp.concatenate([skv[:, :, :, ks].reshape(cached, HD), fresh[:, ks], pad], axis=0)
        values = jnp.concatenate([skv[:, :, :, vs].reshape(cached, HD), fresh[:, vs], pad], axis=0)
        rows = qown[:, g * kvd : (g + 1) * kvd].astype(BF)
        rows = rows.reshape(4 * kvd * tile, HD)
        scores = lax.dot_general(
            rows, keys, (((1,), (1,)), ((), ())), preferred_element_type=F32
        ) * SCALE
        cols = scores.shape[1]
        masked = jnp.where(bias < 0, LOW, scores.reshape(4, kvd, tile, cols))
        masked = masked.reshape(scores.shape)
        top = jnp.max(masked, axis=1, keepdims=True)
        weights = jnp.exp(masked - top)
        total = jnp.sum(weights, axis=1, keepdims=True)
        out = jnp.dot(weights.astype(BF), values, preferred_element_type=F32) / total
        out = out.astype(tdt).reshape(4, kvd, tile, HD)
        lane = lax.broadcasted_iota(jnp.int32, (rows.shape[0], HD), 1)
        st = jnp.where(lane == 0, top, jnp.where(lane == 1, total, 0.0))
        st = st.reshape(4, kvd, tile, HD)
        for hq in range(kvd):
            j = g * kvd + hq
            sbuf[j] = out[:, hq]
            block = st[:, hq].reshape(4 * tile, HD)
            block = jnp.concatenate([block, jnp.zeros((HD - 4 * tile, HD), F32)], axis=0)
            sstat[j] = block.T[0:8]

    def own_copy(j, source):
        return (
            pltpu.make_async_remote_copy(
                src_ref=sbuf.at[j], dst_ref=srecv.at[source], send_sem=d_s.at[j],
                recv_sem=d_r.at[source], device_id={"decode": j}, device_id_type=MESH),
            pltpu.make_async_remote_copy(
                src_ref=sstat.at[j], dst_ref=ssrecv.at[source], send_sem=e_s.at[j],
                recv_sem=e_r.at[source], device_id={"decode": j}, device_id_type=MESH),
        )

    for step in range(1, nb):
        for part in range(2):
            q_copy(part, step).wait()
            if step + 1 < nb:
                q_copy(part, step + 1).start()
    peers = [lax.rem(me + k, nd) for k in range(1, nd)]
    for j in peers:
        for copy in own_copy(j, me):
            copy.start()
    srecv[me] = sbuf[me]
    ssrecv[me] = sstat[me]

    g_head = me // kvd

    def out_copy(hq, p, slot):
        return pltpu.make_async_remote_copy(
            src_ref=obuf.at[hq, p], dst_ref=orecv.at[slot, p],
            send_sem=o_s.at[hq, p], recv_sem=o_r.at[slot, p],
            device_id={"decode": g_mine * kvd + hq}, device_id_type=MESH)

    def stat_copy(hq, slot):
        return pltpu.make_async_remote_copy(
            src_ref=stat.at[hq], dst_ref=strecv.at[slot],
            send_sem=t_s.at[hq], recv_sem=t_r.at[slot],
            device_id={"decode": g_mine * kvd + hq}, device_id_type=MESH)

    turns = [lax.rem(pair + 1 + k, kvd) for k in range(kvd)]
    for load in loads[3:5]:
        load.wait()
    for which in range(2):
        kv_send(which).wait()
    m_rows = nd * kvd * tile
    lane = lax.broadcasted_iota(jnp.int32, (m_rows, HD), 1)
    st = jnp.zeros((m_rows, HD), F32)
    positions = 2 * kv.shape[2]
    for p in range(4):
        keys = kv[:, p, :, 0:HD].reshape(positions, HD)
        values = kv[:, p, :, HD : 2 * HD].reshape(positions, HD)
        rows = qall[(p // 2,) + (slice(None),) * nb + (p % 2,)].astype(BF).reshape(m_rows, HD)
        scores = lax.dot_general(
            rows, keys, (((1,), (1,)), ((), ())), preferred_element_type=F32
        ) * SCALE
        top = jnp.max(scores, axis=1, keepdims=True)
        weights = jnp.exp(scores - top)
        total = jnp.sum(weights, axis=1, keepdims=True)
        out = jnp.dot(weights.astype(BF), values, preferred_element_type=F32) / total
        out = out.astype(tdt).reshape(nd, kvd, tile, HD)
        for hq in range(kvd):
            obuf[hq, p] = out[:, hq]
        st = jnp.where(lane == 2 * p, top, jnp.where(lane == 2 * p + 1, total, st))
        for hq in turns:

            @pl.when(g_mine * kvd + hq != me)
            def _():
                out_copy(hq, p, pair).start()

    st = st.reshape(nd, kvd, tile, HD)
    for hq in range(kvd):
        stat[hq] = st[:, hq].reshape(nd * tile, HD).T[0:8]
    for hq in turns:

        @pl.when(g_mine * kvd + hq != me)
        def _():
            stat_copy(hq, pair).start()

        @pl.when(g_mine * kvd + hq == me)
        def _():
            orecv[pair] = obuf[hq]
            strecv[pair] = stat[hq]

    for j in peers:
        for copy in own_copy(j, j):
            copy.wait()
    for slot in range(nd // 2):

        @pl.when(2 * slot + g_head != me)
        def _():
            for p in range(4):
                out_copy(0, p, slot).wait_recv()
            stat_copy(0, slot).wait_recv()

    for hq in range(kvd):

        @pl.when(g_mine * kvd + hq != me)
        def _():
            for p in range(4):
                out_copy(hq, p, pair).wait_send()
            stat_copy(hq, pair).wait_send()

    nc = nd // 2
    turned = jnp.concatenate(
        [strecv[...].reshape(nc * 8, HD), ssrecv[...].reshape(nd * 8, HD), jnp.zeros((nd * 4, HD), F32)],
        axis=0,
    ).T
    merged = []
    for p in range(4):
        tops = [turned[:, b * 8 + 2 * p : b * 8 + 2 * p + 1] for b in range(nc)]
        sums = [turned[:, b * 8 + 2 * p + 1 : b * 8 + 2 * p + 2] for b in range(nc)]
        span = slice(p * tile, (p + 1) * tile)
        ats = [(nc + d) * 8 for d in range(nd)]
        tops.append(jnp.concatenate([turned[span, at : at + 1] for at in ats], axis=0))
        sums.append(jnp.concatenate([turned[span, at + 1 : at + 2] for at in ats], axis=0))
        best = functools.reduce(jnp.maximum, tops)
        whole = jnp.zeros_like(best)
        joined = jnp.zeros((nd * tile, HD), F32)
        for b in range(nc + 1):
            factor = jnp.exp(tops[b] - best) * sums[b]
            if b < nc:
                piece = orecv[b, p].reshape(nd * tile, HD)
            else:
                piece = jnp.concatenate([srecv[d, p] for d in range(nd)], axis=0)
            whole = whole + factor
            joined = joined + factor * piece.astype(F32)
        merged.append((joined / whole).astype(BF))
    merged = jnp.concatenate(merged, axis=0)
    row = lax.broadcasted_iota(jnp.int32, (nd * 16, 4 * nd * tile), 0)
    col = lax.broadcasted_iota(jnp.int32, (nd * 16, 4 * nd * tile), 1)
    at = (row // 4) % 4 * (nd * tile) + row // 16 * tile + row % 4
    picked = []
    for h in range(hpd):
        select = jnp.where(col == at + h * 4, 1.0, 0.0).astype(BF)
        picked.append(jnp.dot(select, merged, preferred_element_type=F32).astype(BF))
    attention = jnp.concatenate(picked, axis=1)

    loads[5].wait()
    loads[6].wait()
    width = wo.shape[1]
    half = width // 2
    cube = (2,) * nb
    s_orders = [dims[-1:] + dims[:-1][::-1], dims[-1:] + dims[:-1]]

    def p_copy(part, step):
        tail = (slice(None), slice(part * half, (part + 1) * half))
        return scatter_copy(
            acc, lands[part][step], dims, s_orders[part], step, tail,
            p_s.at[part, step], p_r.at[part, step],
        )

    for part in range(2):
        for c in range(part * half, (part + 1) * half, 512):
            part_sum = jnp.dot(attention, wo[:, c : c + 512], preferred_element_type=F32)
            acc[(slice(None),) * (nb + 1) + (slice(c, c + 512),)] = part_sum.astype(BF).reshape(cube + (16, 512))
        p_copy(part, 0).start()
    for step in range(nb):
        for part in range(2):
            p_copy(part, step).wait()
            span = slice(part * half, (part + 1) * half)
            at = cube_index(dims, set(s_orders[part][: step + 1])) + (slice(None), span)
            summed = acc[at].astype(F32) + lands[part][step][...].astype(F32)
            if step + 1 < nb:
                acc[at] = summed.astype(BF)
                p_copy(part, step + 1).start()
            else:
                hidden = [hid_ref[p, :, span].astype(F32) for p in range(4)]
                res_ref[:, span] = jnp.concatenate(hidden, axis=0) + summed
    residual = res_ref[...]
    scale = lax.rsqrt(jnp.mean(residual * residual, axis=1, keepdims=True) + 1e-06)
    pay_ref[:, 0:width] = (residual * scale * gain_ref[...]).astype(BF)
    routes = jnp.concatenate([ids_ref[...].astype(F32), gates_ref[...]], axis=0)
    routes = jnp.concatenate([routes, jnp.zeros((16, HD - 16), F32)], axis=1)
    routes = jnp.concatenate([routes, jnp.zeros((HD - 16, HD), F32)], axis=0).T[0:16]
    ids, gates = routes[:, 0:TOPK], routes[:, TOPK : 2 * TOPK]
    lane = lax.broadcasted_iota(jnp.int32, (16, HD), 1).astype(F32)
    table = jnp.zeros((16, HD), F32)
    for k in range(TOPK):
        table = jnp.where(lane == ids[:, k : k + 1], gates[:, k : k + 1], table)
    high = table.astype(BF)
    pay_ref[:, width : width + HD] = high
    pay_ref[:, width + HD :] = (table - high.astype(F32)).astype(BF)


def expert_kernel(
    np_, nd, pay_ref, res_ref, wg_ref, wu_ref, wd_ref, out_ref, xbuf, wg, wu, wd, zland, held, *rest
):
    nb = nbits(nd)
    lands = [rest[:nb], rest[nb : 2 * nb]]
    local_sem, g_s, g_r, r_s, r_r, z_s, z_r, y_s, y_r = rest[2 * nb :]
    dims = [("decode", k) for k in range(nb - 1, -1, -1)]
    orders = [dims, dims[:-1][::-1] + dims[-1:]]
    mine = cube_index(dims, set(dims))
    width = res_ref.shape[1]
    full = pay_ref.shape[1]
    half = width // 2
    spans = [slice(0, half), slice(half, width)]
    loads = [
        pltpu.make_async_copy(wg_ref.at[0], wg, local_sem.at[0]),
        pltpu.make_async_copy(wu_ref.at[0], wu, local_sem.at[1]),
        pltpu.make_async_copy(wd_ref.at[0], wd, local_sem.at[2]),
    ]
    for load in loads:
        load.start()

    def across(k):
        bits = [bit_of("prompt", b) for b in range(nbits(np_))]
        bits = [1 - bit if (k >> b) % 2 else bit for b, bit in enumerate(bits)]
        return {"prompt": sum(bit * (1 << b) for b, bit in enumerate(bits))}

    barrier = pltpu.get_barrier_semaphore()
    for dim in dims:
        pl.semaphore_signal(barrier, inc=1, device_id=partner(*dim), device_id_type=MESH)
    for k in range(1, np_):
        pl.semaphore_signal(barrier, inc=1, device_id=across(k), device_id_type=MESH)
    xbuf[(0,) + mine] = pay_ref[...]
    pl.semaphore_wait(barrier, nb + np_ - 1)

    def z_in(k):
        return pltpu.make_async_remote_copy(
            src_ref=pay_ref, dst_ref=xbuf.at[(k,) + mine], send_sem=z_s.at[k], recv_sem=z_r.at[k],
            device_id=across(k), device_id_type=MESH)

    def z_out(k):
        return pltpu.make_async_remote_copy(
            src_ref=xbuf.at[(k,) + mine + (slice(None), slice(0, width))], dst_ref=zland.at[k],
            send_sem=y_s.at[k], recv_sem=y_r.at[k], device_id=across(k), device_id_type=MESH)

    def gather(k, part, step):
        tail = (slice(None), slice(part * full // 2, (part + 1) * full // 2))
        return gather_copy(
            xbuf.at[k], dims, orders[part], step, tail, g_s.at[k, part, step], g_r.at[k, part, step]
        )

    def scatter(k, part, step):
        return scatter_copy(
            xbuf.at[k], lands[part][step].at[k], dims, orders[part][::-1], step,
            (slice(None), spans[part]), r_s.at[k, part, step], r_r.at[k, part, step],
        )

    expert = lax.axis_index("prompt") * nd + lax.axis_index("decode")
    m = nd * 16
    cube = (2,) * nb

    def activate(k):
        x = xbuf[(k,) + (slice(None),) * (nb + 1) + (slice(0, width),)].reshape(m, width)
        gated = jnp.dot(x, wg[...], preferred_element_type=F32)
        lifted = jnp.dot(x, wu[...], preferred_element_type=F32)
        return (gated / (1.0 + jnp.exp(-gated)) * lifted).astype(BF)

    def project(k, act):
        at = (k,) + (slice(None),) * (nb + 1)
        gates = xbuf[at + (slice(width, full),)].reshape(m, full - width).astype(F32)
        both = gates[:, 0:HD] + gates[:, HD:]
        lane = lax.broadcasted_iota(jnp.int32, both.shape, 1)
        gate = jnp.sum(jnp.where(lane == expert, both, 0.0), axis=1, keepdims=True)
        for part in range(2):
            for c in range(part * half, (part + 1) * half, 1024):
                y = jnp.dot(act, wd[:, c : c + 1024], preferred_element_type=F32)
                y = jnp.where(gate > 0, gate * y, 0.0).astype(BF)
                xbuf[at + (slice(c, c + 1024),)] = y.reshape(cube + (16, 1024))
            scatter(k, part, 0).start()

    def reduce(k, step):
        for part in range(2):
            scatter(k, part, step - 1).wait()
            at = (k,) + cube_index(dims, set(orders[part][::-1][:step])) + (slice(None), spans[part])
            summed = xbuf[at].astype(F32) + lands[part][step - 1][k].astype(F32)
            if step == nb and k == 0:
                res_ref_sum = res_ref[:, spans[part]] + summed
                for other in range(1, np_):
                    if part == 0:
                        z_out(other).wait()
                    res_ref_sum = res_ref_sum + zland[other, :, spans[part]].astype(F32)
                for p in range(4):
                    out_ref[p, :, spans[part]] = res_ref_sum[4 * p : 4 * p + 4].astype(BF)
            else:
                xbuf[at] = summed.astype(BF)
                if step < nb:
                    scatter(k, part, step).start()
        if step == nb and k > 0:
            z_out(k).start()

    for k in range(1, np_):
        z_in(k).start()
    for tick in range(1 + 2 * nb + np_):
        for k in range(np_):
            step = tick - k
            if 0 <= step <= nb:
                if step == 0 and k > 0:
                    z_in(k).wait()
                for part in range(2):
                    if step > 0:
                        gather(k, part, step - 1).wait()
                    if step < nb:
                        gather(k, part, step).start()
        now = tick - 1 - nb
        if now == -1:
            loads[0].wait()
            loads[1].wait()
            held[...] = activate(0)
        if 0 <= now < np_:
            if now == 0:
                loads[2].wait()
            block = (now + 1) % np_
            project(block, activate(block) if block else held[...])
        for turn in range(np_):
            step = now - turn
            if 1 <= step <= nb:
                reduce((turn + 1) % np_, step)


def per_device(
    np_, nd, hidden_in, queries, new_kv, prompt_kv, sample_kv, counts, out_proj, norm_gain,
    expert_ids, expert_gates, w_gate, w_up, w_down,
):
    prompts, samples, width = hidden_in.shape
    rows = prompts * samples
    hpd = out_proj.shape[0] // HD
    tile = hpd * samples
    groups = H // hpd
    tdt = BF if tile % 16 == 0 else F32
    vmem = pl.BlockSpec(memory_space=pltpu.VMEM)
    hbm = pl.BlockSpec(memory_space=pl.ANY)

    nb = nbits(nd)
    half = width // 2
    cube = (2,) * nb
    dma = pltpu.SemaphoreType.DMA

    def turn(table):
        return table.transpose(0, 1, 3, 2).reshape(TOPK, rows)

    lands = [pltpu.VMEM((2,) * (nb - 1 - step) + (16, half), BF) for step in range(nb)]
    residual, payload = pl.pallas_call(
        functools.partial(attention_kernel, nd, hpd, tdt),
        out_shape=(
            jax.ShapeDtypeStruct((rows, width), F32),
            jax.ShapeDtypeStruct((rows, width + 256), BF),
        ),
        in_specs=[hbm, hbm, hbm, hbm, vmem, hbm, hbm, vmem, vmem, vmem],
        out_specs=(vmem, vmem),
        scratch_shapes=[
            pltpu.VMEM(queries.shape, BF),
            pltpu.VMEM(new_kv.shape, BF),
            pltpu.VMEM(hidden_in.shape, BF),
            pltpu.VMEM((prompts, groups, tile, HD), tdt),
            pltpu.VMEM((2,) + cube + (2, groups // 2, tile, HD), tdt),
            pltpu.VMEM((2, prompts, prompt_kv.shape[1], 2 * HD), BF),
            pltpu.VMEM(sample_kv.shape, BF),
            pltpu.VMEM(out_proj.shape, BF),
            pltpu.VMEM((nd // 2, prompts, nd, tile, HD), tdt),
            pltpu.VMEM((nd // 2, prompts, nd, tile, HD), tdt),
            pltpu.VMEM((nd, prompts, tile, HD), tdt),
            pltpu.VMEM((nd, prompts, tile, HD), tdt),
            pltpu.VMEM((nd // 2, 8, HD), F32),
            pltpu.VMEM((nd // 2, 8, HD), F32),
            pltpu.VMEM((nd, 8, HD), F32),
            pltpu.VMEM((nd, 8, HD), F32),
            pltpu.VMEM(cube + (16, width), BF),
        ]
        + lands
        + lands
        + [dma((7,)), dma((2, nb)), dma((2, nb)), dma((2,)), dma((2,))]
        + [dma((nd // 2, 4)), dma((nd // 2, 4)), dma((nd // 2,)), dma((nd // 2,))]
        + [dma((nd,)) for _ in range(4)]
        + [dma((2, nb)), dma((2, nb))],
        compiler_params=pltpu.CompilerParams(
            collective_id=0, has_side_effects=True, vmem_limit_bytes=62 * 2**20
        ),
        name="attention",
    )(
        queries, prompt_kv, sample_kv, new_kv, counts, out_proj, hidden_in,
        norm_gain.reshape(1, width), turn(expert_ids), turn(expert_gates),
    )

    lands = [pltpu.VMEM((np_,) + (2,) * (nb - 1 - step) + (16, half), BF) for step in range(nb)]
    return pl.pallas_call(
        functools.partial(expert_kernel, np_, nd),
        out_shape=jax.ShapeDtypeStruct(hidden_in.shape, BF),
        in_specs=[vmem, vmem, hbm, hbm, hbm],
        out_specs=vmem,
        scratch_shapes=[
            pltpu.VMEM((np_,) + cube + (16, width + 256), BF),
            pltpu.VMEM(w_gate.shape[1:], BF),
            pltpu.VMEM(w_up.shape[1:], BF),
            pltpu.VMEM(w_down.shape[1:], BF),
            pltpu.VMEM((np_, rows, width), BF),
            pltpu.VMEM((nd * rows, w_gate.shape[2]), BF),
        ]
        + lands
        + lands
        + [dma((3,))] + [dma((np_, 2, nb)) for _ in range(4)] + [dma((np_,)) for _ in range(4)],
        compiler_params=pltpu.CompilerParams(
            collective_id=1, has_side_effects=True, vmem_limit_bytes=62 * 2**20
        ),
        name="experts",
    )(payload, residual, w_gate, w_up, w_down)


def solution(mesh):
    in_specs = (
        P("prompt", "decode", None),
        P("prompt", "decode", None),
        P("prompt", "decode", None),
        P("prompt", "decode", None),
        P("prompt", "decode", None, None),
        P("prompt", "decode"),
        P("decode", None),
        P(),
        P("prompt", "decode", None, None),
        P("prompt", "decode", None, None),
        P(("prompt", "decode"), None, None),
        P(("prompt", "decode"), None, None),
        P(("prompt", "decode"), None, None),
    )
    return jax.shard_map(
        functools.partial(per_device, mesh.shape["prompt"], mesh.shape["decode"]),
        mesh=mesh, in_specs=in_specs, out_specs=P("prompt", "decode", None), check_vma=False,
    )
```
